128 devices in a mesh: wide: 32 (over x, z, y_hi), narrow: 4 (over y_lo, core).
Axes of the slice: x: 4, y: 4 (y_hi: 2, y_lo: 2; y = y_hi * 2 + y_lo), z: 4, core: 2. Of those that a mesh axis runs over, the one named last changes fastest.
Arguments:
- homolog_embedding: bfloat16 [128, 5120, 256], P(('wide', 'narrow')), may hold values from -6 to 6
- presence_flags: float32 [128, 5120], P(('wide', 'narrow')), may hold values from 0.1 to 1
- standardizer_scaling: float32 [256], replicated, may hold values from 0.1 to 1.9
- standardizer_offset: float32 [256], replicated, may hold values from -3 to 3
- first_factor_coefficients: bfloat16 [256, 32], replicated, may hold values from -0.375 to 0.375
- first_factor_offset: float32 [32], replicated, may hold values from -3 to 3
- second_factor_coefficients: bfloat16 [256, 32], replicated, may hold values from -0.375 to 0.375
- second_factor_offset: float32 [32], replicated, may hold values from -3 to 3
- final_coefficients: bfloat16 [1024, 128], replicated, may hold values from -0.5 to 0.5
Outputs:
- pair_update: bfloat16 [1024, 5120, 128], P('wide', 'narrow')
The draws below stay inside these ranges and needn't reach their ends.
All inputs are finite; a program needn't handle non-finite values.
Results may differ from the reference program's by a relative error of at most 0.0054.
Values may be sent and summed in bfloat16 or wider, within the bound.
No kernel may reach another device: no remote copies, remote signals or barrier semaphores. Data moves between devices by JAX's collectives and lax.ppermute only.
A program may use at most 128 MiB of HBM per device.

```python
import jax
import jax.numpy as jnp
from jax import lax

FEATURE_COUNT = 256
HIDDEN_WIDTH = 32
CZ = 128
AMINO_ACID_COUNT = 5120
HOMOLOG_COUNT = 128
RD = 32
N_WIDE = 32


def block_scale(stream_key, shape, split, low, largest):
    factor_of = 1.0
    for position, parts in split:
        heights = jax.random.uniform(jax.random.fold_in(jax.random.fold_in(stream_key, 6), position), (parts,), jnp.float32, low / len(split), largest / len(split))
        factor_of = factor_of * jnp.repeat(jnp.exp(heights), shape[position] // parts).reshape((-1,) + (1,) * (len(shape) - 1 - position))
    return factor_of


def gaussian(key, extent, scale, limit, shards=(), held_as=jnp.bfloat16):
    drawn = scale * jax.random.normal(key, extent, jnp.float32)
    if shards:
        drawn = drawn * block_scale(key, extent, shards, -0.22, 0.18)
    return jnp.clip(drawn, -limit, limit).astype(held_as)


def setup_inputs(seed: int = 0) -> dict:
    streams_of = jax.random.split(jax.random.key(seed), 10)
    homolog_embedding = gaussian(streams_of[0], (HOMOLOG_COUNT, AMINO_ACID_COUNT, FEATURE_COUNT), 1.0, 6.0, ((0, 128),))
    presence_flags = jnp.clip(0.1 + 0.9 * jax.random.uniform(streams_of[1], (HOMOLOG_COUNT, AMINO_ACID_COUNT), jnp.float32) ** block_scale(streams_of[1], (HOMOLOG_COUNT, AMINO_ACID_COUNT), ((0, 128),), -0.2, 0.2), 0.1, 1.0)
    standardizer_scaling = jnp.clip(1.0 + 0.18 * jax.random.normal(streams_of[2], (FEATURE_COUNT,), jnp.float32), 0.1, 1.9)
    standardizer_offset = gaussian(streams_of[3], (FEATURE_COUNT,), 0.5, 3.0, (), jnp.float32)
    first_factor_coefficients = gaussian(streams_of[4], (FEATURE_COUNT, HIDDEN_WIDTH), FEATURE_COUNT ** -0.5, 0.375)
    first_factor_offset = gaussian(streams_of[5], (HIDDEN_WIDTH,), 0.5, 3.0, (), jnp.float32)
    second_factor_coefficients = gaussian(streams_of[6], (FEATURE_COUNT, HIDDEN_WIDTH), FEATURE_COUNT ** -0.5, 0.375)
    second_factor_offset = gaussian(streams_of[7], (HIDDEN_WIDTH,), 0.5, 3.0, (), jnp.float32)
    final_coefficients = gaussian(streams_of[8], (HIDDEN_WIDTH * HIDDEN_WIDTH, CZ), (HIDDEN_WIDTH * HIDDEN_WIDTH // 8) ** -0.5, 0.5)
    return {"homolog_embedding": homolog_embedding, "presence_flags": presence_flags, "standardizer_scaling": standardizer_scaling, "standardizer_offset": standardizer_offset, "first_factor_coefficients": first_factor_coefficients, "first_factor_offset": first_factor_offset, "second_factor_coefficients": second_factor_coefficients, "second_factor_offset": second_factor_offset, "final_coefficients": final_coefficients}


def reference(homolog_embedding, presence_flags, standardizer_scaling, standardizer_offset, first_factor_coefficients, first_factor_offset, second_factor_coefficients, second_factor_offset, final_coefficients):
    rows_all = RD * N_WIDE
    collected_presence = presence_flags.astype(jnp.float32)
    rounded_presence = collected_presence.astype(jnp.bfloat16)

    def affine_transform(packed):
        seq_rows, seq_mask = packed
        payload_elements = seq_rows.astype(jnp.float32)
        centre = lax.optimization_barrier(jnp.mean(payload_elements, axis=-1, keepdims=True))
        spread = lax.optimization_barrier(jnp.mean((payload_elements - centre) ** 2, axis=-1, keepdims=True))
        standardized_embedding = ((payload_elements - centre) * lax.rsqrt(spread + 1e-05) * standardizer_scaling + standardizer_offset).astype(jnp.bfloat16)
        left_part = (jnp.dot(standardized_embedding[:rows_all], first_factor_coefficients, preferred_element_type=jnp.float32) + first_factor_offset) * seq_mask[:rows_all, None]
        right_part = (jnp.dot(standardized_embedding, second_factor_coefficients, preferred_element_type=jnp.float32) + second_factor_offset) * seq_mask[:, None]
        return (left_part.astype(jnp.bfloat16), right_part.astype(jnp.bfloat16))
    first_factor_embeddings, second_factor_embeddings = lax.map(affine_transform, (homolog_embedding, collected_presence))
    count = jnp.dot(rounded_presence[:, :rows_all].T, rounded_presence, preferred_element_type=jnp.float32)
    right_wide = second_factor_embeddings.astype(jnp.float32)
    weight_wide = final_coefficients.astype(jnp.float32)
    block = 8

    def pair_block(index):
        start = (index * block).astype(jnp.int32)
        left_blk = lax.dynamic_slice_in_dim(first_factor_embeddings, start, block, 1).astype(jnp.float32)
        outer = jnp.einsum('sic,sje->ijce', left_blk, right_wide).astype(jnp.bfloat16)
        outer = lax.optimization_barrier(outer).astype(jnp.float32)
        mixed = jnp.dot(outer.reshape(block * AMINO_ACID_COUNT, HIDDEN_WIDTH * HIDDEN_WIDTH), weight_wide).reshape(block, AMINO_ACID_COUNT, CZ)
        count_blk = lax.dynamic_slice_in_dim(count, start, block, 0)
        return (mixed / (0.001 + count_blk[:, :, None])).astype(jnp.bfloat16)
    blocks = lax.map(pair_block, jnp.arange(rows_all // block, dtype=jnp.int32))
    return blocks.reshape(rows_all, AMINO_ACID_COUNT, CZ)
```

```python
import jax
import jax.numpy as jnp
from jax import lax
from jax.experimental import pallas as pl
from jax.experimental.pallas import tpu as pltpu
from jax.sharding import Mesh
from jax.sharding import PartitionSpec as P

RD = 32
CHUNK = 256
GROUP = 8
COLUMN = ("yh", "yl", "core")
PLANE = ("x", "z", "yh")
EVERY = ("x", "z", "yh", "yl", "core")
OFFSETS = (0, -1, 1, 2)
f32 = jnp.float32
bf16 = jnp.bfloat16


def vmem(mib):
    return pltpu.CompilerParams(vmem_limit_bytes=mib * 2**20)


def whole(*shape):
    return pl.BlockSpec(shape, lambda *_: (0,) * len(shape))


def project(x, mask, gain, bias, w_left, b_left, w_right, b_right):
    rows, features = x.shape
    quarter = rows // 4
    width = w_right.shape[0]
    left_rows = RD * 32
    sub = 256

    def kernel(x_ref, m_ref, g_ref, s_ref, wl_ref, bl_ref, wr_ref, br_ref, left_ref, right_ref):
        step = pl.program_id(0)
        for part in range(quarter // sub):
            at = slice(part * sub, (part + 1) * sub)
            v = x_ref[at, :].astype(f32)
            centre = jnp.mean(v, axis=-1, keepdims=True)
            v = v - centre
            spread = jnp.mean(v * v, axis=-1, keepdims=True)
            normed = (v * lax.rsqrt(spread + 1e-05) * g_ref[...] + s_ref[...]).astype(bf16)
            m = m_ref[0, :, at]

            def affine(w_ref, b_ref):
                y = lax.dot_general(
                    w_ref[...], normed, (((1,), (1,)), ((), ())), preferred_element_type=f32
                )
                return (y + b_ref[...]) * m

            y = affine(wr_ref, br_ref).astype(bf16)
            right_ref[0, 0, :, at] = y
            right_ref[1, 0, :, at] = y
            if (part + 1) * sub <= left_rows:

                @pl.when(step == 0)
                def _():
                    left_ref[at, :] = affine(wl_ref, bl_ref).T.astype(bf16)

    return pl.pallas_call(
        kernel,
        grid=(4,),
        out_shape=(
            jax.ShapeDtypeStruct((left_rows, width), bf16),
            jax.ShapeDtypeStruct((2, 4, width, quarter), bf16),
        ),
        in_specs=[
            pl.BlockSpec((quarter, features), lambda q: (q, 0)),
            pl.BlockSpec((1, 1, quarter), lambda q: (q, 0, 0)),
            whole(1, features),
            whole(1, features),
            whole(width, features),
            whole(width, 1),
            whole(width, features),
            whole(width, 1),
        ],
        out_specs=(whole(left_rows, width), pl.BlockSpec((2, 1, width, quarter), lambda q: (0, q, 0, 0))),
        compiler_params=vmem(40),
        name="project",
    )(x, mask.reshape(4, 1, quarter), gain, bias, w_left, b_left, w_right, b_right)


def ring(step):
    return [(i, (i + step) % 4) for i in range(4)]


def gather_ring(block, axis, low, high):
    before = lax.ppermute(block, axis, ring(1))
    after = lax.ppermute(block, axis, ring(-1))
    far_low = lax.ppermute(low(before), axis, ring(1))
    far_high = lax.ppermute(high(after), axis, ring(-1))
    return block, before, after, far_low, far_high


def interleave(first, second):
    columns = first[0].shape[-1]
    chunks = columns // CHUNK
    rows = 16 * 32

    def kernel(*refs):
        ins, outs, scratch = refs[:10], refs[10:12], refs[12]
        for half in range(2):
            own, before, after, low, high = ins[5 * half : 5 * half + 5]
            for place in range(4):
                for m in range(8):
                    if place < 3:
                        part = (own, before, after)[place][m]
                    else:
                        part = low[m] if m < 4 else high[m - 4]
                    part = part.astype(f32)
                    for lane in range(CHUNK // 128):
                        at = pl.ds(place * 8 + m, 16, stride=32)
                        scratch[half, lane, at, :] = part[:, lane * 128 : (lane + 1) * 128]
            for lane in range(CHUNK // 128):
                for eh in range(2):
                    block = scratch[half, lane, eh * 256 : (eh + 1) * 256, :].astype(bf16)
                    outs[half][eh, 0, :, lane * 128 : (lane + 1) * 128] = block

    full = pl.BlockSpec((8, 16, CHUNK), lambda j: (0, 0, j))
    part = pl.BlockSpec((4, 16, CHUNK), lambda j: (0, 0, j))
    out = jax.ShapeDtypeStruct((2, chunks, 256, CHUNK), bf16)
    return pl.pallas_call(
        kernel,
        grid=(chunks,),
        out_shape=(out, out),
        in_specs=[full, full, full, part, part] * 2,
        out_specs=(pl.BlockSpec((2, 1, 256, CHUNK), lambda j: (0, j, 0, 0)),) * 2,
        scratch_shapes=[pltpu.VMEM((2, CHUNK // 128, rows, 128), f32)],
        compiler_params=vmem(40),
        name="interleave",
    )(*first, *second)


def pair(left1, left2, weight, count, first, second):
    chunks = first[0].shape[1]
    out_width = weight.shape[0]

    def kernel(l1, l2, w_ref, n_ref, *refs):
        ins, out_ref, outer = refs[:10], refs[10], refs[11]

        def rows_of(group, _):
            at = pl.ds(pl.multiple_of(group * (GROUP * 32), GROUP * 32), GROUP * 32)
            for e in range(32):
                half, eh, e8 = e // 16, (e // 8) % 2, e % 8
                own, before, after, low, high = ins[5 * half : 5 * half + 5]
                s = slice(e8 * 32, e8 * 32 + 32)
                far = high if eh else low
                right = jnp.concatenate(
                    [own[eh, 0, s, :], before[eh, 0, s, :], after[eh, 0, s, :], far[0, s, :]], axis=0
                )
                prod = jnp.dot((l1, l2)[half][at, :], right, preferred_element_type=f32).astype(bf16)
                for i in range(GROUP):
                    outer[i, e * 32 : (e + 1) * 32, :] = prod[i * 32 : (i + 1) * 32, :]
            scale = 1.0 / (0.001 + n_ref[0, pl.ds(pl.multiple_of(group * GROUP, GROUP), GROUP), :])
            for i in range(GROUP):
                mixed = jnp.dot(w_ref[...], outer[i], preferred_element_type=f32)
                out_ref[group * GROUP + i] = (mixed * scale[i : i + 1, :]).T.astype(bf16)
            return 0

        lax.fori_loop(0, RD // GROUP, rows_of, 0)

    big = pl.BlockSpec((2, 1, 256, CHUNK), lambda j: (0, j, 0, 0))
    part = pl.BlockSpec((1, 256, CHUNK), lambda j: (j, 0, 0))
    return pl.pallas_call(
        kernel,
        grid=(chunks,),
        out_shape=jax.ShapeDtypeStruct((RD, chunks * CHUNK, out_width), bf16),
        in_specs=[
            whole(*left1.shape),
            whole(*left2.shape),
            whole(*weight.shape),
            pl.BlockSpec((1, RD, CHUNK), lambda j: (j, 0, 0)),
        ]
        + [big, big, big, part, part] * 2,
        out_specs=pl.BlockSpec((RD, CHUNK, out_width), lambda j: (0, j, 0)),
        scratch_shapes=[pltpu.VMEM((GROUP, 1024, CHUNK), bf16)],
        compiler_params=vmem(56),
        name="pair",
    )(left1, left2, weight, count, *first, *second)


def sequence_orders():
    x, z = lax.axis_index("x"), lax.axis_index("z")
    k = jnp.arange(128, dtype=jnp.int32)
    offsets = jnp.array(OFFSETS, jnp.int32)
    slow, fast, m = offsets[k // 32], offsets[(k // 8) % 4], k % 8
    first = ((x + fast) % 4) * 32 + ((z + slow) % 4) * 8 + m
    second = ((x + slow) % 4) * 32 + ((z + fast) % 4) * 8 + m
    return first, second


def on_device(x, mask, gain, bias, w_left, b_left, w_right, b_right, w_out):
    columns = x.shape[1] // 4
    width = w_left.shape[1]
    chunks = columns // CHUNK
    plane = lax.axis_index(PLANE)
    narrow = lax.axis_index(("yl", "core"))

    masks = lax.all_gather(mask.astype(bf16), EVERY, axis=0, tiled=True)

    left, right = project(
        x[0], mask, gain[None], bias[None], w_left.T, b_left[:, None], w_right.T, b_right[:, None]
    )
    right = right.reshape(8, width, columns)
    right = lax.all_to_all(right, COLUMN, 0, 0, tiled=True)

    halves = right[:, :16], right[:, 16:]
    lower, upper = (lambda t: t[:4]), (lambda t: t[4:])
    first = gather_ring(halves[0], "x", lower, upper)
    second = gather_ring(halves[1], "z", lower, upper)
    one, two = interleave(first, second)
    lower, upper = (lambda t: t[0]), (lambda t: t[1])
    first = gather_ring(one, "z", lower, upper)
    second = gather_ring(two, "x", lower, upper)

    left = lax.all_to_all(left.reshape(32, RD, width), PLANE, 0, 0, tiled=True)
    left = lax.all_gather(left, ("yl", "core"), axis=1)
    left = left.reshape(128, RD * width)
    order = jnp.concatenate(sequence_orders())
    choose = (jnp.arange(128, dtype=jnp.int32)[:, None] == order[None, :]).astype(bf16)
    left = lax.dot_general(left, choose, (((0,), (0,)), ((), ())), preferred_element_type=f32).astype(bf16)

    row_masks = lax.dynamic_slice_in_dim(masks, plane * RD, RD, 1)
    column_masks = lax.dynamic_slice_in_dim(masks, narrow * columns, columns, 1)
    count = jnp.einsum("si,sj->ij", row_masks, column_masks, preferred_element_type=f32)
    count = count.reshape(RD, chunks, CHUNK).transpose(1, 0, 2)

    weight = w_out.reshape(width, width, -1).transpose(2, 1, 0).reshape(-1, width * width)
    return pair(left[:, :128], left[:, 128:], weight, count, first, second)


def solution(mesh):
    split = Mesh(mesh.devices.reshape(4, 4, 2, 2, 2), EVERY)
    placed = (P(EVERY, None, None), P(EVERY, None)) + (P(),) * 7
    return jax.shard_map(
        on_device,
        mesh=split,
        in_specs=placed,
        out_specs=P(PLANE, ("yl", "core"), None),
        check_vma=False,
    )
```

```python
import jax
import jax.numpy as jnp
from jax import lax
from jax.experimental import pallas as pl
from jax.experimental.pallas import tpu as pltpu
from jax.sharding import Mesh
from jax.sharding import PartitionSpec as P

RD = 32
CHUNK = 256
GROUP = 8
TILE = 128
COLUMN = ("yh", "yl", "core")
PLANE = ("x", "z", "yh")
EVERY = ("x", "z", "yh", "yl", "core")
f32 = jnp.float32
bf16 = jnp.bfloat16


def vmem(mib=60):
    return pltpu.CompilerParams(vmem_limit_bytes=mib * 2**20)


def whole(*shape):
    return pl.BlockSpec(shape, lambda *_: (0,) * len(shape))


def turned(bias_ref):
    return jnp.broadcast_to(bias_ref[...], (8, bias_ref.shape[1])).T[:, :1]


def standardize(v, gain, bias):
    v = v.astype(f32)
    v = v - jnp.mean(v, axis=-1, keepdims=True)
    spread = jnp.mean(v * v, axis=-1, keepdims=True)
    return (v * lax.rsqrt(spread + 1e-05) * gain + bias).astype(bf16)


def affine(w_ref, bias, normed, mask):
    y = lax.dot_general(w_ref[...], normed, (((1,), (1,)), ((), ())), preferred_element_type=f32)
    return (y + bias) * mask


def project_left(x, mask, gain, bias, weight, shift):
    features = x.shape[1]
    width = weight.shape[0]
    rows = RD * 32
    half = width // 2
    sub = 512

    def kernel(x_ref, m_ref, g_ref, s_ref, w_ref, b_ref, out_ref, mask_ref):
        b = turned(b_ref)
        y = []
        for part in range(rows // sub):
            at = slice(part * sub, (part + 1) * sub)
            normed = standardize(x_ref[at, :], g_ref[...], s_ref[...])
            y.append(affine(w_ref, b, normed, m_ref[:, at]))
        y = jnp.concatenate(y, axis=1)

        def piece(v, px, pz, yh):
            first = (px * 8 + pz * 2 + yh) * RD
            return v[:, first : first + RD]

        for yh in range(2):
            masks = []
            for slow in range(4):
                at = slice(slow * TILE, (slow + 1) * TILE)
                one = [piece(y[:half], slow, fast, yh) for fast in range(4)]
                two = [piece(y[half:], fast, slow, yh) for fast in range(4)]
                out_ref[yh, :half, at] = jnp.concatenate(one, axis=1).astype(bf16)
                out_ref[yh, half:, at] = jnp.concatenate(two, axis=1).astype(bf16)
                masks.append(jnp.concatenate([piece(m_ref[...], slow, fast, yh) for fast in range(4)], axis=1))
            masks = jnp.concatenate(masks + [jnp.zeros((4, TILE), f32)], axis=0)
            mask_ref[yh] = masks

    return pl.pallas_call(
        kernel,
        grid=(1,),
        out_shape=(
            jax.ShapeDtypeStruct((2, width, 4 * TILE), bf16),
            jax.ShapeDtypeStruct((2, 8, TILE), f32),
        ),
        in_specs=[
            pl.BlockSpec((rows, features), lambda _: (0, 0)),
            pl.BlockSpec((1, rows), lambda _: (0, 0)),
            whole(1, features),
            whole(1, features),
            whole(width, features),
            whole(1, width),
        ],
        out_specs=(whole(2, width, 4 * TILE), whole(2, 8, TILE)),
        compiler_params=vmem(),
        name="project_left",
    )(x, mask, gain, bias, weight, shift)


def project_right(x, mask, gain, bias, weight, shift, left, left_mask):
    rows, features = x.shape
    quarter = rows // 4
    width = weight.shape[0]
    sub = 640
    total = quarter + 5 * TILE

    def kernel(x_ref, m_ref, g_ref, s_ref, w_ref, b_ref, l_ref, n_ref, out_ref):
        b = turned(b_ref)
        for part in range(quarter // sub):
            at = slice(part * sub, (part + 1) * sub)
            normed = standardize(x_ref[at, :], g_ref[...], s_ref[...])
            y = affine(w_ref, b, normed, m_ref[0, :, at]).astype(bf16)
            out_ref[0, 0, :, at] = y
            out_ref[1, 0, :, at] = y
        m = [m_ref[0, :, k * TILE : (k + 1) * TILE] for k in range(quarter // TILE)]
        zeros = jnp.zeros((width - len(m) - 4, TILE), f32)
        for yh in range(2):
            tile = jnp.concatenate(m + [n_ref[yh, :4, :], zeros], axis=0)
            out_ref[yh, 0, :, quarter : quarter + TILE] = tile.astype(bf16)
            out_ref[yh, 0, :, quarter + TILE :] = l_ref[yh]

    return pl.pallas_call(
        kernel,
        grid=(4,),
        out_shape=jax.ShapeDtypeStruct((2, 4, width, total), bf16),
        in_specs=[
            pl.BlockSpec((quarter, features), lambda q: (q, 0)),
            pl.BlockSpec((1, 1, quarter), lambda q: (q, 0, 0)),
            whole(1, features),
            whole(1, features),
            whole(width, features),
            whole(1, width),
            whole(*left.shape),
            whole(*left_mask.shape),
        ],
        out_specs=pl.BlockSpec((2, 1, width, total), lambda q: (0, q, 0, 0)),
        compiler_params=vmem(),
        name="project_right",
    )(x, mask.reshape(4, 1, quarter), gain, bias, weight, shift, left, left_mask)


def ring(step):
    return [(i, (i + step) % 4) for i in range(4)]


def interleave(position, first, second, columns, start, chunks, with_left):
    tiles = CHUNK // TILE
    mask_tile = columns // TILE
    sizes = (8, 8, 8, 4, 4)
    heights = (544, 512)
    extra = (272, 256) if with_left else (0, 0)

    def place_rows(ins, put):
        own, before, after, low, high = ins
        for place in range(4):
            for m in range(8):
                if place < 3:
                    part = (own, before, after)[place][m]
                else:
                    part = low[m] if m < 4 else high[m - 4]
                put(pl.ds(place * 8 + m, 16, stride=32), part.astype(f32))

    def kernel(pos, *refs):
        main, masks, lefts = refs[:10], refs[10:15], refs[15:-4]
        outs, (scratch, mask_rows) = refs[-4:-2], refs[-2:]

        def put_mask(at, part):
            mask_rows[at, :] = part

        place_rows(masks, put_mask)

        def masks_at(row):
            return mask_rows[pl.ds(pl.multiple_of(row * 32, 32), 32), :].astype(bf16)

        for chunk in range(chunks):
            for half in range(2):
                base = chunk * heights[half]

                def put(at, part):
                    for lane in range(tiles):
                        scratch[chunk, half, lane, at, :] = part[:, lane * TILE : (lane + 1) * TILE]

                ins = [r.at[:, :, chunk * CHUNK : (chunk + 1) * CHUNK] for r in main[5 * half : 5 * half + 5]]
                place_rows(ins, put)
                for lane in range(tiles):
                    at = slice(lane * TILE, (lane + 1) * TILE)
                    outs[half][base : base + 512, at] = scratch[chunk, half, lane].astype(bf16)
                    if half == 0:
                        outs[0][base + 512 : base + 544, at] = masks_at((start + chunk) * tiles + lane)
        if with_left:
            for half in range(2):
                base = chunks * heights[half]

                def put_left(at, part):
                    scratch[chunks, half, 0, at, :] = part

                place_rows(lefts[5 * half : 5 * half + 5], put_left)
                for lane in range(2):
                    at = slice(lane * TILE, (lane + 1) * TILE)
                    rows = scratch[chunks, half, 0, lane * 256 : (lane + 1) * 256, :]
                    outs[half][base : base + 256, at] = rows.astype(bf16)
            rows = masks_at(mask_tile + pos[0])
            base = chunks * heights[0] + 256
            outs[0][base : base + 16, :TILE] = rows[:16]
            outs[0][base : base + 16, TILE:] = rows[16:]

    def blocks(m):
        span = chunks * CHUNK
        if start * CHUNK % span == 0:
            return pl.BlockSpec((m, 16, span), lambda _, pos: (0, 0, start * CHUNK // span))
        return pl.BlockSpec((pl.Element(m), pl.Element(16), pl.Element(span)), lambda _, pos: (0, 0, start * CHUNK))

    def mask_blocks(m):
        return pl.BlockSpec((m, 16, TILE), lambda _, pos: (0, 0, mask_tile))

    def left_blocks(m, half):
        return pl.BlockSpec((m, 16, TILE), lambda _, pos: (0, 0, mask_tile + 1 + pos[half]))

    specs = [blocks(m) for m in sizes] * 2 + [mask_blocks(m) for m in sizes]
    args = (*first, *second, *first)
    if with_left:
        specs += [left_blocks(m, half) for half in range(2) for m in sizes]
        args += (*first, *second)
    shapes = [(chunks * heights[half] + extra[half], CHUNK) for half in range(2)]
    return pl.pallas_call(
        kernel,
        grid_spec=pltpu.PrefetchScalarGridSpec(
            num_scalar_prefetch=1,
            grid=(1,),
            in_specs=specs,
            out_specs=tuple(whole(*shape) for shape in shapes),
            scratch_shapes=[
                pltpu.VMEM((chunks + with_left, 2, tiles, 512, TILE), f32),
                pltpu.VMEM((512, TILE), f32),
            ],
        ),
        out_shape=tuple(jax.ShapeDtypeStruct(shape, bf16) for shape in shapes),
        compiler_params=vmem(),
        name="interleave",
    )(position, *args)


def arrange_left(position, first, second, chunks):
    def kernel(pos, *refs):
        ins, (one_ref, two_ref, mask_ref, scratch) = refs[:10], refs[10:]

        def sequences(half, rows, lane):
            at = slice(lane * TILE, (lane + 1) * TILE)
            own, before, after, low, high = ins[5 * half : 5 * half + 5]
            return [r[rows, at] for r in (own, before, after)] + [(low, high)[lane][rows, :]]

        def mine(half, values):
            wanted = lax.broadcasted_iota(jnp.int32, (RD, TILE), 0) + RD * pos[1 - half]
            pick = (lax.broadcasted_iota(jnp.int32, (RD, TILE), 1) == wanted).astype(bf16)
            return lax.dot_general(pick, values, (((1,), (1,)), ((), ())), preferred_element_type=f32)

        for half in range(2):
            for c in range(16):
                lane, row = divmod(c, 8)
                values = sequences(half, slice(row * 32, row * 32 + 32), lane)
                values = mine(half, jnp.concatenate(values, axis=0))
                scratch[pl.ds(half * 16 + c, RD, stride=32), :] = values
        masks = [sequences(0, slice(256, 272), lane) for lane in range(2)]
        masks = [masks[lane][place] for place in range(4) for lane in range(2)]
        mask_ref[...] = mine(0, jnp.concatenate(masks, axis=0)).astype(bf16)

        held = scratch[...].astype(bf16)
        k = lax.broadcasted_iota(jnp.int32, (128, 128), 0)
        swapped = (k // 8 % 4) * 32 + k // 32 * 8 + k % 8
        swap = (lax.broadcasted_iota(jnp.int32, (128, 128), 1) == swapped).astype(bf16)
        other = jnp.dot(held, swap, preferred_element_type=f32)
        own_order = lax.broadcasted_iota(jnp.int32, (RD * 32, 128), 0) % 32 < 16
        one_ref[...] = jnp.where(own_order, scratch[...], other).astype(bf16)
        two_ref[...] = jnp.where(own_order, other, scratch[...]).astype(bf16)

    def block(half, t):
        rows = (272, 256)[half]
        return pl.BlockSpec((rows, t.shape[1]), lambda _, pos: (2 * chunks, 0))

    shapes = [(RD * 32, 128), (RD * 32, 128), (RD, 128)]
    return pl.pallas_call(
        kernel,
        grid_spec=pltpu.PrefetchScalarGridSpec(
            num_scalar_prefetch=1,
            grid=(1,),
            in_specs=[block(0, t) for t in first] + [block(1, t) for t in second],
            out_specs=tuple(whole(*shape) for shape in shapes),
            scratch_shapes=[pltpu.VMEM((RD * 32, 128), f32)],
        ),
        out_shape=tuple(jax.ShapeDtypeStruct(shape, bf16) for shape in shapes),
        compiler_params=vmem(),
        name="arrange_left",
    )(position, *first, *second)


def pair(left1, left2, weight, row_mask, first, second, base, start, chunks, result, columns):
    out_width = weight.shape[0]
    skip = start - base
    earlier = () if result is None else (result,)

    def kernel(l1, l2, w_ref, n_ref, *refs):
        ins, (out_ref, outer, scale) = refs[:10], refs[-3:]

        def sequences(half, row):
            own, before, after, low, high = ins[5 * half : 5 * half + 5]
            at = slice(row * 32, row * 32 + 32)
            far = jnp.concatenate([low[at, :], high[at, :]], axis=1)
            return jnp.concatenate([own[at, :], before[at, :], after[at, :], far], axis=0)

        count = jnp.dot(n_ref[...], sequences(0, 16), preferred_element_type=f32)
        scale[...] = 1.0 / (0.001 + count)

        def rows_of(group, _):
            at = pl.ds(pl.multiple_of(group * (GROUP * 32), GROUP * 32), GROUP * 32)
            for e in range(32):
                left = (l1, l2)[e // 16][at, :]
                prod = jnp.dot(left, sequences(e // 16, e % 16), preferred_element_type=f32).astype(bf16)
                for i in range(GROUP):
                    outer[i, e * 32 : (e + 1) * 32, :] = prod[i * 32 : (i + 1) * 32, :]
            part = scale[pl.ds(pl.multiple_of(group * GROUP, GROUP), GROUP), :]
            for i in range(GROUP):
                mixed = jnp.dot(w_ref[...], outer[i], preferred_element_type=f32)
                out_ref[group * GROUP + i] = (mixed * part[i : i + 1, :]).T.astype(bf16)
            return 0

        lax.fori_loop(0, RD // GROUP, rows_of, 0)

    blocks = [pl.BlockSpec((544, t.shape[1]), lambda j: (skip + j, 0)) for t in first]
    blocks += [pl.BlockSpec((512, t.shape[1]), lambda j: (skip + j, 0)) for t in second]
    return pl.pallas_call(
        kernel,
        grid=(chunks,),
        out_shape=jax.ShapeDtypeStruct((RD, columns, out_width), bf16),
        in_specs=[
            whole(*left1.shape),
            whole(*left2.shape),
            whole(*weight.shape),
            whole(*row_mask.shape),
        ]
        + blocks
        + [pl.BlockSpec(memory_space=pl.ANY)] * len(earlier),
        out_specs=pl.BlockSpec((RD, CHUNK, out_width), lambda j: (0, start + j, 0)),
        scratch_shapes=[pltpu.VMEM((GROUP, 1024, CHUNK), bf16), pltpu.VMEM((RD, CHUNK), f32)],
        input_output_aliases={14: 0} if earlier else {},
        compiler_params=vmem(),
        name="pair",
    )(left1, left2, weight, row_mask, *first, *second, *earlier)


def send_both(blocks):
    return [
        (lax.ppermute(block, axis, ring(1)), lax.ppermute(block, axis, ring(-1))) for block, axis in blocks
    ]


def send_on(parts):
    return [
        (lax.ppermute(low, axis, ring(1)), lax.ppermute(high, axis, ring(-1))) for (low, high), axis in parts
    ]


def on_device(x, mask, gain, bias, w_left, b_left, w_right, b_right, w_out):
    columns = x.shape[1] // 4
    width = w_left.shape[1]
    chunks = columns // CHUNK
    together = lax.optimization_barrier

    position = jnp.stack([lax.axis_index("x"), lax.axis_index("z")]).astype(jnp.int32)
    norm = gain[None], bias[None]
    left = project_left(x[0], mask, *norm, w_left.T, b_left[None])
    right = project_right(x[0], mask, *norm, w_right.T, b_right[None], *left)
    right = lax.all_to_all(right.reshape(8, width, -1), COLUMN, 0, 0, tiled=True)

    halves = right[:, :16], right[:, 16:]
    got = send_both(((halves[0], "x"), (halves[1], "z")))
    far = send_on([((before[:4], after[4:]), axis) for (before, after), axis in zip(got, "xz")])
    held = [(halves[h], *got[h], *far[h]) for h in range(2)]

    mixed = [
        interleave(position, *held, columns, 0, 2, True),
        interleave(position, *held, columns, 2, chunks - 2, False),
    ]
    weight = w_out.reshape(width, width, -1).transpose(2, 1, 0).reshape(-1, width * width)

    def own_step(blocks):
        got = send_both(((blocks[0], "z"), (blocks[1], "x")))
        return got, [(before[:, :TILE], after[:, TILE:]) for before, after in got]

    def all_places(blocks, got, far):
        return [(blocks[h], *got[h], *far[h]) for h in range(2)]

    early, late = mixed
    got, onward = own_step(early)
    onward, late = together((onward, late))
    far = send_on(list(zip(onward, "zx")))
    far, late = together((far, late))
    early = all_places(early, got, far)
    got, onward = own_step(late)

    left1, left2, row_mask = arrange_left(position, *early, 2)
    fixed = left1, left2, weight, row_mask
    result = pair(*fixed, *early, 0, 0, 1, None, columns)
    onward, result = together((onward, result))
    far = send_on(list(zip(onward, "zx")))
    late = all_places(late, got, far)
    result = pair(*fixed, *early, 0, 1, 1, result, columns)
    return pair(*fixed, *late, 2, 2, chunks - 2, result, columns)


def solution(mesh):
    split = Mesh(mesh.devices.reshape(4, 4, 2, 2, 2), EVERY)
    placed = (P(EVERY, None, None), P(EVERY, None)) + (P(),) * 7
    return jax.shard_map(
        on_device,
        mesh=split,
        in_specs=placed,
        out_specs=P(PLANE, ("yl", "core"), None),
        check_vma=False,
    )
```

```python
import jax
import jax.numpy as jnp
from jax import lax
from jax.experimental import pallas as pl
from jax.experimental.pallas import tpu as pltpu
from jax.sharding import Mesh
from jax.sharding import PartitionSpec as P

RD = 32
CHUNK = 256
GROUP = 32
TILE = 128
COLUMN = ("yh", "yl", "core")
PLANE = ("x", "z", "yh")
EVERY = ("x", "z", "yh", "yl", "core")
f32 = jnp.float32
bf16 = jnp.bfloat16


def vmem(mib=63):
    return pltpu.CompilerParams(vmem_limit_bytes=mib * 2**20)


def whole(*shape):
    return pl.BlockSpec(shape, lambda *_: (0,) * len(shape))


def turned(bias_ref):
    return jnp.broadcast_to(bias_ref[...], (8, bias_ref.shape[1])).T[:, :1]


def standardize(v, gain, bias):
    v = v.astype(f32)
    v = v - jnp.mean(v, axis=-1, keepdims=True)
    spread = jnp.mean(v * v, axis=-1, keepdims=True)
    return (v * lax.rsqrt(spread + 1e-05) * gain + bias).astype(bf16)


def affine(w_ref, bias, normed, mask):
    y = lax.dot_general(w_ref[...], normed, (((1,), (1,)), ((), ())), preferred_element_type=f32)
    return (y + bias) * mask


def project_left(x, mask, gain, bias, weight, shift):
    features = x.shape[1]
    width = weight.shape[0]
    rows = RD * 32
    half = width // 2
    sub = 512

    def kernel(x_ref, m_ref, g_ref, s_ref, w_ref, b_ref, out_ref, mask_ref):
        b = turned(b_ref)
        y = []
        for part in range(rows // sub):
            at = slice(part * sub, (part + 1) * sub)
            normed = standardize(x_ref[at, :], g_ref[...], s_ref[...])
            y.append(affine(w_ref, b, normed, m_ref[:, at]))
        y = jnp.concatenate(y, axis=1)

        def piece(v, px, pz, yh):
            first = (px * 8 + pz * 2 + yh) * RD
            return v[:, first : first + RD]

        for yh in range(2):
            masks = []
            for slow in range(4):
                at = slice(slow * TILE, (slow + 1) * TILE)
                one = [piece(y[:half], slow, fast, yh) for fast in range(4)]
                two = [piece(y[half:], fast, slow, yh) for fast in range(4)]
                out_ref[yh, :half, at] = jnp.concatenate(one, axis=1).astype(bf16)
                out_ref[yh, half:, at] = jnp.concatenate(two, axis=1).astype(bf16)
                masks.append(jnp.concatenate([piece(m_ref[...], slow, fast, yh) for fast in range(4)], axis=1))
            masks = jnp.concatenate(masks + [jnp.zeros((4, TILE), f32)], axis=0)
            mask_ref[yh] = masks

    return pl.pallas_call(
        kernel,
        grid=(1,),
        out_shape=(
            jax.ShapeDtypeStruct((2, width, 4 * TILE), bf16),
            jax.ShapeDtypeStruct((2, 8, TILE), f32),
        ),
        in_specs=[
            pl.BlockSpec((rows, features), lambda _: (0, 0)),
            pl.BlockSpec((1, rows), lambda _: (0, 0)),
            whole(1, features),
            whole(1, features),
            whole(width, features),
            whole(1, width),
        ],
        out_specs=(whole(2, width, 4 * TILE), whole(2, 8, TILE)),
        compiler_params=vmem(),
        name="project_left",
    )(x, mask, gain, bias, weight, shift)


def project_right(x, mask, gain, bias, weight, shift, left, left_mask):
    rows, features = x.shape
    quarter = rows // 4
    width = weight.shape[0]
    sub = 640
    total = quarter + 5 * TILE

    def kernel(x_ref, m_ref, g_ref, s_ref, w_ref, b_ref, l_ref, n_ref, out_ref):
        b = turned(b_ref)
        for part in range(quarter // sub):
            at = slice(part * sub, (part + 1) * sub)
            normed = standardize(x_ref[at, :], g_ref[...], s_ref[...])
            y = affine(w_ref, b, normed, m_ref[0, :, at]).astype(bf16)
            out_ref[0, 0, :, at] = y
            out_ref[1, 0, :, at] = y
        m = [m_ref[0, :, k * TILE : (k + 1) * TILE] for k in range(quarter // TILE)]
        zeros = jnp.zeros((width - len(m) - 4, TILE), f32)
        for yh in range(2):
            tile = jnp.concatenate(m + [n_ref[yh, :4, :], zeros], axis=0)
            out_ref[yh, 0, :, quarter : quarter + TILE] = tile.astype(bf16)
            out_ref[yh, 0, :, quarter + TILE :] = l_ref[yh]

    return pl.pallas_call(
        kernel,
        grid=(4,),
        out_shape=jax.ShapeDtypeStruct((2, 4, width, total), bf16),
        in_specs=[
            pl.BlockSpec((quarter, features), lambda q: (q, 0)),
            pl.BlockSpec((1, 1, quarter), lambda q: (q, 0, 0)),
            whole(1, features),
            whole(1, features),
            whole(width, features),
            whole(1, width),
            whole(*left.shape),
            whole(*left_mask.shape),
        ],
        out_specs=pl.BlockSpec((2, 1, width, total), lambda q: (0, q, 0, 0)),
        compiler_params=vmem(),
        name="project_right",
    )(x, mask.reshape(4, 1, quarter), gain, bias, weight, shift, left, left_mask)


def ring(step):
    return [(i, (i + step) % 4) for i in range(4)]


def interleave(position, first, second, columns, start, chunks, with_left):
    tiles = CHUNK // TILE
    mask_tile = columns // TILE
    sizes = (8, 8, 8, 4, 4)
    heights = (544, 512)
    extra = (272, 256) if with_left else (0, 0)

    def by_row(ins, lane):
        own, before, after, low, high = ins
        at = slice(lane * TILE, (lane + 1) * TILE)
        parts = [own[:, :, at], before[:, :, at], after[:, :, at], low[:, :, at], high[:, :, at]]
        near = jnp.swapaxes(jnp.concatenate(parts[:2], axis=0), 0, 1)
        away = jnp.swapaxes(jnp.concatenate(parts[2:], axis=0), 0, 1)
        return jnp.concatenate([near, away], axis=1).reshape(512, TILE)

    def kernel(pos, *refs):
        main, masks, lefts = refs[:10], refs[10:15], refs[15 : 15 + 10 * with_left]
        outs, mask_rows = refs[15 + 10 * with_left : -1], refs[-1]

        def put(half, lane, base, rows):
            outs[half][base : base + rows.shape[0], lane * TILE : (lane + 1) * TILE] = rows

        mask_rows[...] = by_row(masks, 0)
        for chunk in range(chunks):
            for half in range(2):
                base = chunk * heights[half]
                for lane in range(tiles):
                    put(half, lane, base, by_row(main[5 * half : 5 * half + 5], chunk * tiles + lane))
                    if half == 0:
                        row = ((start + chunk) * tiles + lane) * 32
                        put(0, lane, base + 512, mask_rows[row : row + 32, :])
        if with_left:
            for half in range(2):
                rows = by_row(lefts[5 * half : 5 * half + 5], 0)
                for lane in range(2):
                    put(half, lane, chunks * heights[half], rows[lane * 256 : (lane + 1) * 256])
            rows = mask_rows[pl.ds(pl.multiple_of((mask_tile + pos[0]) * 32, 32), 32), :]
            for lane in range(2):
                put(0, lane, chunks * heights[0] + 256, rows[lane * 16 : (lane + 1) * 16])

    def blocks(m):
        span = chunks * CHUNK
        if start * CHUNK % span == 0:
            return pl.BlockSpec((m, 16, span), lambda _, pos: (0, 0, start * CHUNK // span))
        return pl.BlockSpec((pl.Element(m), pl.Element(16), pl.Element(span)), lambda _, pos: (0, 0, start * CHUNK))

    def mask_blocks(m):
        return pl.BlockSpec((m, 16, TILE), lambda _, pos: (0, 0, mask_tile))

    def left_blocks(m, half):
        return pl.BlockSpec((m, 16, TILE), lambda _, pos: (0, 0, mask_tile + 1 + pos[half]))

    specs = [blocks(m) for m in sizes] * 2 + [mask_blocks(m) for m in sizes]
    args = (*first, *second, *first)
    if with_left:
        specs += [left_blocks(m, half) for half in range(2) for m in sizes]
        args += (*first, *second)
    shapes = [(chunks * heights[half] + extra[half], CHUNK) for half in range(2)]
    return pl.pallas_call(
        kernel,
        grid_spec=pltpu.PrefetchScalarGridSpec(
            num_scalar_prefetch=1,
            grid=(1,),
            in_specs=specs,
            out_specs=tuple(whole(*shape) for shape in shapes),
            scratch_shapes=[pltpu.VMEM((512, TILE), bf16)],
        ),
        out_shape=tuple(jax.ShapeDtypeStruct(shape, bf16) for shape in shapes),
        compiler_params=vmem(),
        name="interleave",
    )(position, *args)


def arrange_left(position, first, second, chunks, w_out):
    width = 32
    features, out_width = w_out.shape

    def kernel(pos, *refs):
        ins, (w_ref, one_ref, two_ref, mask_ref, weight_ref, scratch) = refs[:8], refs[8:]
        w = jnp.swapaxes(w_ref[...].reshape(width, width, out_width), 0, 1).reshape(features, out_width)
        weight_ref[...] = w.T

        def sequences(half, rows, lane):
            at = slice(lane * TILE, (lane + 1) * TILE)
            return [r[rows, at] for r in ins[4 * half : 4 * half + 4]]

        def mine(half, values):
            wanted = lax.broadcasted_iota(jnp.int32, (RD, TILE), 0) + RD * pos[1 - half]
            pick = (lax.broadcasted_iota(jnp.int32, (RD, TILE), 1) == wanted).astype(bf16)
            return lax.dot_general(pick, values, (((1,), (1,)), ((), ())), preferred_element_type=f32)

        for half in range(2):
            for c in range(16):
                lane, row = divmod(c, 8)
                values = sequences(half, slice(row * 32, row * 32 + 32), lane)
                values = mine(half, jnp.concatenate(values, axis=0))
                scratch[pl.ds(half * 16 + c, RD, stride=32), :] = values
        masks = [sequences(0, slice(256, 272), lane) for lane in range(2)]
        masks = [masks[lane][place] for place in range(4) for lane in range(2)]
        mask_ref[...] = mine(0, jnp.concatenate(masks, axis=0)).astype(bf16)

        held = scratch[...].astype(bf16)
        k = lax.broadcasted_iota(jnp.int32, (128, 128), 0)
        swapped = (k // 8 % 4) * 32 + k // 32 * 8 + k % 8
        swap = (lax.broadcasted_iota(jnp.int32, (128, 128), 1) == swapped).astype(bf16)
        other = jnp.dot(held, swap, preferred_element_type=f32)
        own_order = lax.broadcasted_iota(jnp.int32, (RD * 32, 128), 0) % 32 < 16
        one_ref[...] = jnp.where(own_order, scratch[...], other).astype(bf16)
        two_ref[...] = jnp.where(own_order, other, scratch[...]).astype(bf16)

    def block(half, t):
        rows = (272, 256)[half]
        return pl.BlockSpec((rows, t.shape[1]), lambda _, pos: (2 * chunks, 0))

    shapes = [(RD * 32, 128), (RD * 32, 128), (RD, 128), (out_width, features)]
    return pl.pallas_call(
        kernel,
        grid_spec=pltpu.PrefetchScalarGridSpec(
            num_scalar_prefetch=1,
            grid=(1,),
            in_specs=[block(0, t) for t in first] + [block(1, t) for t in second] + [whole(*w_out.shape)],
            out_specs=tuple(whole(*shape) for shape in shapes),
            scratch_shapes=[pltpu.VMEM((RD * 32, 128), f32)],
        ),
        out_shape=tuple(jax.ShapeDtypeStruct(shape, bf16) for shape in shapes),
        compiler_params=vmem(),
        name="arrange_left",
    )(position, *first, *second, w_out)


def pair(left1, left2, weight, row_mask, first, second, start, chunks, result, columns):
    out_width = weight.shape[0]
    earlier = () if result is None else (result,)

    def kernel(l1, l2, w_ref, n_ref, *refs):
        ins, (out_ref, outer, scale) = refs[:8], refs[-3:]

        def sequences(half, row):
            at = slice(row * 32, row * 32 + 32)
            return jnp.concatenate([r[at, :] for r in ins[4 * half : 4 * half + 4]], axis=0)

        count = jnp.dot(n_ref[...], sequences(0, 16), preferred_element_type=f32)
        scale[...] = 1.0 / (0.001 + count)

        def rows_of(group, _):
            at = pl.ds(pl.multiple_of(group * (GROUP * 32), GROUP * 32), GROUP * 32)
            for e in range(32):
                left = (l1, l2)[e // 16][at, :]
                prod = jnp.dot(left, sequences(e // 16, e % 16), preferred_element_type=f32).astype(bf16)
                for i in range(GROUP):
                    outer[i, e * 32 : (e + 1) * 32, :] = prod[i * 32 : (i + 1) * 32, :]
            part = scale[pl.ds(pl.multiple_of(group * GROUP, GROUP), GROUP), :]
            for i in range(GROUP):
                mixed = jnp.dot(w_ref[...], outer[i], preferred_element_type=f32)
                out_ref[group * GROUP + i] = (mixed * part[i : i + 1, :]).T.astype(bf16)
            return 0

        lax.fori_loop(0, RD // GROUP, rows_of, 0)

    blocks = [pl.BlockSpec((544, t.shape[1]), lambda j: (j, 0)) for t in first]
    blocks += [pl.BlockSpec((512, t.shape[1]), lambda j: (j, 0)) for t in second]
    return pl.pallas_call(
        kernel,
        grid=(chunks,),
        out_shape=jax.ShapeDtypeStruct((RD, columns, out_width), bf16),
        in_specs=[
            whole(*left1.shape),
            whole(*left2.shape),
            whole(*weight.shape),
            whole(*row_mask.shape),
        ]
        + blocks
        + [pl.BlockSpec(memory_space=pl.ANY)] * len(earlier),
        out_specs=pl.BlockSpec((RD, CHUNK, out_width), lambda j: (0, start + j, 0)),
        scratch_shapes=[pltpu.VMEM((GROUP, 1024, CHUNK), bf16), pltpu.VMEM((RD, CHUNK), f32)],
        input_output_aliases={12: 0} if earlier else {},
        compiler_params=vmem(),
        name="pair",
    )(left1, left2, weight, row_mask, *first, *second, *earlier)


def send_both(blocks):
    return [
        (lax.ppermute(block, axis, ring(1)), lax.ppermute(block, axis, ring(-1))) for block, axis in blocks
    ]


def send_on(parts):
    return [
        (lax.ppermute(low, axis, ring(1)), lax.ppermute(high, axis, ring(-1))) for (low, high), axis in parts
    ]


def on_device(x, mask, gain, bias, w_left, b_left, w_right, b_right, w_out):
    columns = x.shape[1] // 4
    width = w_left.shape[1]
    chunks = columns // CHUNK
    together = lax.optimization_barrier

    position = jnp.stack([lax.axis_index("x"), lax.axis_index("z")]).astype(jnp.int32)
    norm = gain[None], bias[None]
    left = project_left(x[0], mask, *norm, w_left.T, b_left[None])
    right = project_right(x[0], mask, *norm, w_right.T, b_right[None], *left)
    right = lax.all_to_all(right.reshape(8, width, -1), COLUMN, 0, 0, tiled=True)

    halves = right[:, :16], right[:, 16:]
    got = send_both(((halves[0], "x"), (halves[1], "z")))
    far = send_on([((before[:4], after[4:]), axis) for (before, after), axis in zip(got, "xz")])
    held = [(halves[h], *got[h], *far[h]) for h in range(2)]

    mixed = [
        interleave(position, *held, columns, 0, 2, True),
        interleave(position, *held, columns, 2, chunks - 2, False),
    ]
    early, late = mixed
    got = send_both(((early[0], "z"), (early[1], "x")))
    got, late = together((got, late))
    far = [lax.ppermute(before, axis, ring(1)) for (before, _), axis in zip(got, "zx")]
    after = [lax.ppermute(block, axis, ring(-1)) for block, axis in zip(late, "zx")]
    far, late = together((far, late))
    early = [(early[h], *got[h], far[h]) for h in range(2)]
    before = [lax.ppermute(block, axis, ring(1)) for block, axis in zip(late, "zx")]
    early, after = together((early, after))
    far = [lax.ppermute(block, axis, ring(-1)) for block, axis in zip(after, "zx")]
    late = [(late[h], before[h], after[h], far[h]) for h in range(2)]

    left1, left2, row_mask, weight = arrange_left(position, *early, 2, w_out)
    fixed = left1, left2, weight, row_mask
    result = pair(*fixed, *early, 0, 2, None, columns)
    return pair(*fixed, *late, 2, chunks - 2, result, columns)


def solution(mesh):
    split = Mesh(mesh.devices.reshape(4, 4, 2, 2, 2), EVERY)
    placed = (P(EVERY, None, None), P(EVERY, None)) + (P(),) * 7
    return jax.shard_map(
        on_device,
        mesh=split,
        in_specs=placed,
        out_specs=P(PLANE, ("yl", "core"), None),
        check_vma=False,
    )
```

```python
import jax
import jax.numpy as jnp
from jax import lax
from jax.experimental import pallas as pl
from jax.experimental.pallas import tpu as pltpu
from jax.sharding import Mesh
from jax.sharding import PartitionSpec as P

RD = 32
CHUNK = 256
GROUP = 32
TILE = 128
COLUMN = ("yh", "yl", "core")
PLANE = ("x", "z", "yh")
EVERY = ("x", "z", "yh", "yl", "core")
f32 = jnp.float32
bf16 = jnp.bfloat16


def vmem(mib=63):
    return pltpu.CompilerParams(vmem_limit_bytes=mib * 2**20)


def whole(*shape):
    return pl.BlockSpec(shape, lambda *_: (0,) * len(shape))


def turned(bias_ref):
    return jnp.broadcast_to(bias_ref[...], (8, bias_ref.shape[1])).T[:, :1]


def standardize(v, gain, bias):
    v = v.astype(f32)
    v = v - jnp.mean(v, axis=-1, keepdims=True)
    spread = jnp.mean(v * v, axis=-1, keepdims=True)
    return (v * lax.rsqrt(spread + 1e-05) * gain + bias).astype(bf16)


def affine(w_ref, bias, normed, mask):
    y = lax.dot_general(w_ref[...], normed, (((1,), (1,)), ((), ())), preferred_element_type=f32)
    return (y + bias) * mask


def one_hot(rows, columns, where):
    row = lax.broadcasted_iota(jnp.int32, (rows, columns), 0)
    column = lax.broadcasted_iota(jnp.int32, (rows, columns), 1)
    return jnp.where(where(row, column), 1.0, 0.0).astype(bf16)


def move(values, choose):
    return jnp.dot(values, choose, preferred_element_type=f32).astype(bf16)


def project_left(x, mask, gain, bias, weight, shift):
    features = x.shape[1]
    width = weight.shape[0]
    rows = RD * 32
    sub = 512

    def kernel(x_ref, m_ref, g_ref, s_ref, w_ref, b_ref, out_ref, mask_ref):
        b = turned(b_ref)
        y = []
        for part in range(rows // sub):
            at = slice(part * sub, (part + 1) * sub)
            normed = standardize(x_ref[at, :], g_ref[...], s_ref[...])
            y.append(affine(w_ref, b, normed, m_ref[:, at]))
        y = jnp.concatenate(y, axis=1)
        y = jnp.concatenate([y, jnp.broadcast_to(m_ref[...], (16, rows))], axis=0).astype(bf16)

        def regroup(src, dst):
            return src == ((dst >> 3) & 3) * 64 + (dst >> 5) * 8 + (dst & 7)

        choose = one_hot(256, 256, regroup)
        y = [move(y[:, k * 256 : (k + 1) * 256], choose) for k in range(4)]
        for device in range(8):
            tile = jnp.concatenate([t[:, device * 32 : (device + 1) * 32] for t in y], axis=1)
            out_ref[device] = tile[:32]
            mask_ref[device] = tile[32:]

    return pl.pallas_call(
        kernel,
        grid=(1,),
        out_shape=(
            jax.ShapeDtypeStruct((8, 32, TILE), bf16),
            jax.ShapeDtypeStruct((8, 16, TILE), bf16),
        ),
        in_specs=[
            pl.BlockSpec((rows, features), lambda _: (0, 0)),
            pl.BlockSpec((1, rows), lambda _: (0, 0)),
            whole(1, features),
            whole(1, features),
            whole(width, features),
            whole(1, width),
        ],
        out_specs=(whole(8, 32, TILE), whole(8, 16, TILE)),
        compiler_params=vmem(),
        name="project_left",
    )(x, mask, gain, bias, weight, shift)


def project_right(x, mask, gain, bias, weight, shift, left, left_mask):
    rows, features = x.shape
    quarter = rows // 4
    width = weight.shape[0]
    sub = 640
    total = quarter + 2 * TILE

    def kernel(x_ref, m_ref, g_ref, s_ref, w_ref, b_ref, l_ref, n_ref, out_ref):
        b = turned(b_ref)
        for part in range(quarter // sub):
            at = slice(part * sub, (part + 1) * sub)
            normed = standardize(x_ref[at, :], g_ref[...], s_ref[...])
            y = affine(w_ref, b, normed, m_ref[0, :, at]).astype(bf16)
            out_ref[0, 0, :, at] = y
            out_ref[1, 0, :, at] = y
        m = [m_ref[0, :, k * TILE : (k + 1) * TILE] for k in range(quarter // TILE)]
        for yh in range(2):
            device = yh * 4 + pl.program_id(0)
            tile = jnp.concatenate(m + [jnp.zeros((16 - len(m), TILE), f32)], axis=0)
            out_ref[yh, 0, :16, quarter : quarter + TILE] = tile.astype(bf16)
            out_ref[yh, 0, 16:, quarter : quarter + TILE] = n_ref[device]
            out_ref[yh, 0, :, quarter + TILE :] = l_ref[device]

    return pl.pallas_call(
        kernel,
        grid=(4,),
        out_shape=jax.ShapeDtypeStruct((2, 4, width, total), bf16),
        in_specs=[
            pl.BlockSpec((quarter, features), lambda q: (q, 0)),
            pl.BlockSpec((1, 1, quarter), lambda q: (q, 0, 0)),
            whole(1, features),
            whole(1, features),
            whole(width, features),
            whole(1, width),
            whole(*left.shape),
            whole(*left_mask.shape),
        ],
        out_specs=pl.BlockSpec((2, 1, width, total), lambda q: (0, q, 0, 0)),
        compiler_params=vmem(),
        name="project_right",
    )(x, mask.reshape(4, 1, quarter), gain, bias, weight, shift, left, left_mask)


def ring(step):
    return [(i, (i + step) % 4) for i in range(4)]


def interleave(position, first, second, columns, start, chunks, w_out=None):
    tiles = CHUNK // TILE
    sizes = (8, 8, 8, 4, 4)
    heights = (544, 512)
    extra = 0 if w_out is not None else 144
    width = 32
    mask_tile = columns // TILE

    def by_row(ins, lane):
        own, before, after, low, high = ins
        at = slice(lane * TILE, (lane + 1) * TILE)
        parts = [own[:, :, at], before[:, :, at], after[:, :, at], low[:, :, at], high[:, :, at]]
        near = jnp.swapaxes(jnp.concatenate(parts[:2], axis=0), 0, 1)
        away = jnp.swapaxes(jnp.concatenate(parts[2:], axis=0), 0, 1)
        return jnp.concatenate([near, away], axis=1).reshape(512, TILE)

    def kernel(pos, *refs):
        main, masks, rest, outs = refs[:10], refs[10:15], refs[15:-3], refs[-3:]
        mask_rows = by_row(masks, 0)
        for chunk in range(chunks):
            for half in range(2):
                base = chunk * heights[half]
                for lane in range(tiles):
                    at = slice(lane * TILE, (lane + 1) * TILE)
                    rows = by_row(main[5 * half : 5 * half + 5], chunk * tiles + lane)
                    outs[half][base : base + 512, at] = rows
                    if half == 0:
                        row = ((start + chunk) * tiles + lane) * 32
                        outs[0][base + 512 : base + 544, at] = mask_rows[row : row + 32, :]
        if w_out is not None:
            w = rest[0][...].reshape(width, width, TILE)
            outs[2][...] = jnp.swapaxes(w, 0, 1).reshape(width * width, TILE).T
            return

        def mine(group):
            def pick(src, dst):
                place = ((dst >> 3) & 3) * 32 + pos[1] * 8 + (dst & 7)
                return (src == place) & ((dst >> 5) == group)

            return one_hot(TILE, TILE, pick)

        choose = [mine(group) for group in range(4)]
        left_masks, *lefts = [by_row(rest[5 * k : 5 * k + 5], 0) for k in range(3)]
        for lane, rows in enumerate(lefts):
            at = slice(lane * TILE, (lane + 1) * TILE)
            parts = [rows[g * 128 : (g + 1) * 128] for g in range(4)]
            parts = [jnp.dot(v, c, preferred_element_type=f32) for v, c in zip(parts, choose)]
            outs[2][:128, at] = sum(parts[1:], parts[0]).astype(bf16)
            outs[2][128:, at] = move(left_masks[lane * 16 : (lane + 1) * 16], choose[0])
        outs[1][chunks * 512 :, :] = outs[2][...]

    def blocks(m):
        span = chunks * CHUNK
        if start * CHUNK % span == 0:
            return pl.BlockSpec((m, 16, span), lambda _, pos: (0, 0, start * CHUNK // span))
        return pl.BlockSpec((pl.Element(m), pl.Element(16), pl.Element(span)), lambda _, pos: (0, 0, start * CHUNK))

    def tile_blocks(m, tile):
        return pl.BlockSpec((m, 16, TILE), lambda _, pos: (0, 0, tile))

    specs = [blocks(m) for m in sizes] * 2 + [tile_blocks(m, mask_tile) for m in sizes]
    args = (*first, *second, *first)
    shapes = [(chunks * heights[0], CHUNK), (chunks * heights[1] + extra, CHUNK)]
    if w_out is None:
        specs += [tile_blocks(m, mask_tile + k) for k in (0, 2, 1) for m in sizes]
        args += (*second, *second, *second)
        shapes.append((extra, CHUNK))
    else:
        specs.append(whole(*w_out.shape))
        args += (w_out,)
        shapes.append((w_out.shape[1], width * width))
    return pl.pallas_call(
        kernel,
        grid_spec=pltpu.PrefetchScalarGridSpec(
            num_scalar_prefetch=1,
            grid=(1,),
            in_specs=specs,
            out_specs=tuple(whole(*shape) for shape in shapes),
        ),
        out_shape=tuple(jax.ShapeDtypeStruct(shape, bf16) for shape in shapes),
        compiler_params=vmem(),
        name="interleave",
    )(position, *args)


def arrange_left(position, own, before, after, far, base):
    height = own.shape[0]

    def kernel(pos, *refs):
        ins, out_ref = refs[:4], refs[4]

        def sequences(rows, lane):
            return [r[rows, lane * TILE : (lane + 1) * TILE] for r in ins]

        def turn(choose, values):
            over = (((1,), (1,)), ((), ()))
            return lax.dot_general(choose, values, over, preferred_element_type=f32).astype(bf16)

        choose = one_hot(32, TILE, lambda row, lane: lane == (row & 3) * 32 + pos[0] * 8 + (row >> 2))
        held = []
        for lane in range(2):
            for c in range(4):
                values = jnp.concatenate(sequences(slice(c * 32, c * 32 + 32), lane), axis=0)
                held.append(turn(choose, values))

        def regroup(dst, src):
            c = dst & 31
            return src == (c >> 4) * 128 + (c & 3) * 32 + (dst >> 5) * 4 + ((c >> 2) & 3)

        held = move(one_hot(256, 256, regroup), jnp.concatenate(held, axis=0))
        swap = one_hot(128, 128, lambda k, to: to == ((k >> 3) & 3) * 32 + (k >> 5) * 8 + (k & 7))
        out_ref[:256, :] = move(held, swap)
        out_ref[256:512, :] = held
        masks = [sequences(slice(128, 144), lane) for lane in range(2)]
        masks = [masks[lane][place] for place in range(4) for lane in range(2)]
        choose = one_hot(16, TILE, lambda row, lane: lane == pos[0] * 8 + row)
        out_ref[512:, :] = move(turn(choose, jnp.concatenate(masks, axis=0)), swap)

    part = pl.BlockSpec((pl.Element(height), pl.Element(CHUNK)), lambda _, pos: (base, 0))
    return pl.pallas_call(
        kernel,
        grid_spec=pltpu.PrefetchScalarGridSpec(
            num_scalar_prefetch=1,
            grid=(1,),
            in_specs=[whole(*own.shape), part, part, whole(*far.shape)],
            out_specs=whole(528, 128),
        ),
        out_shape=jax.ShapeDtypeStruct((528, 128), bf16),
        compiler_params=vmem(),
        name="arrange_left",
    )(position, own, before, after, far)


def pair(left, weight, first, second, start, chunks, result, columns):
    out_width = weight.shape[0]
    earlier = () if result is None else (result,)

    def kernel(left_ref, w_ref, *refs):
        ins = refs[:8]
        out_ref, outer, scale, l1, l2, row_mask = refs[-6:]

        @pl.when(pl.program_id(0) == 0)
        def _():
            for device in range(4):
                at = slice(device * 256, (device + 1) * 256)
                l1[at, :] = left_ref[device, :256, :]
                l2[at, :] = left_ref[device, 256:512, :]
                row_mask[device * 8 : (device + 1) * 8, :] = left_ref[device, 512:, :].astype(f32)[:8]

        def sequences(half, row):
            at = slice(row * 32, row * 32 + 32)
            return jnp.concatenate([r[at, :] for r in ins[4 * half : 4 * half + 4]], axis=0)

        count = jnp.dot(row_mask[...].astype(bf16), sequences(0, 16), preferred_element_type=f32)
        scale[...] = 1.0 / (0.001 + count)

        def rows_of(group, _):
            at = pl.ds(pl.multiple_of(group * (GROUP * 32), GROUP * 32), GROUP * 32)
            for e in range(32):
                left = (l1, l2)[e // 16][at, :]
                prod = jnp.dot(left, sequences(e // 16, e % 16), preferred_element_type=f32).astype(bf16)
                for i in range(GROUP):
                    outer[i, e * 32 : (e + 1) * 32, :] = prod[i * 32 : (i + 1) * 32, :]
            part = scale[pl.ds(pl.multiple_of(group * GROUP, GROUP), GROUP), :]
            for i in range(GROUP):
                mixed = jnp.dot(w_ref[...], outer[i], preferred_element_type=f32)
                out_ref[group * GROUP + i] = (mixed * part[i : i + 1, :]).T.astype(bf16)
            return 0

        lax.fori_loop(0, RD // GROUP, rows_of, 0)

    blocks = [pl.BlockSpec((544, t.shape[1]), lambda j: (j, 0)) for t in first]
    blocks += [pl.BlockSpec((512, t.shape[1]), lambda j: (j, 0)) for t in second]
    return pl.pallas_call(
        kernel,
        grid=(chunks,),
        out_shape=jax.ShapeDtypeStruct((RD, columns, out_width), bf16),
        in_specs=[whole(*left.shape), whole(*weight.shape)]
        + blocks
        + [pl.BlockSpec(memory_space=pl.ANY)] * len(earlier),
        out_specs=pl.BlockSpec((RD, CHUNK, out_width), lambda j: (0, start + j, 0)),
        scratch_shapes=[
            pltpu.VMEM((GROUP, 1024, CHUNK), bf16),
            pltpu.VMEM((RD, CHUNK), f32),
            pltpu.VMEM((1024, 128), bf16),
            pltpu.VMEM((1024, 128), bf16),
            pltpu.VMEM((RD, 128), f32),
        ],
        input_output_aliases={10: 0} if earlier else {},
        compiler_params=vmem(),
        name="pair",
    )(left, weight, *first, *second, *earlier)


def send_both(blocks):
    return [
        (lax.ppermute(block, axis, ring(1)), lax.ppermute(block, axis, ring(-1))) for block, axis in blocks
    ]


def send_on(parts):
    return [
        (lax.ppermute(low, axis, ring(1)), lax.ppermute(high, axis, ring(-1))) for (low, high), axis in parts
    ]


def on_device(x, mask, gain, bias, w_left, b_left, w_right, b_right, w_out):
    columns = x.shape[1] // 4
    width = w_left.shape[1]
    chunks = columns // CHUNK
    together = lax.optimization_barrier

    narrow = ("yl", "core")
    position = jnp.stack([lax.axis_index(axis) for axis in ("x", "z")]).astype(jnp.int32)
    norm = gain[None], bias[None]
    left = project_left(x[0], mask, *norm, w_left.T, b_left[None])
    right = project_right(x[0], mask, *norm, w_right.T, b_right[None], *left)
    right = lax.all_to_all(right.reshape(8, width, -1), COLUMN, 0, 0, tiled=True)

    halves = (
        right[:, :16, : columns + TILE],
        jnp.concatenate([right[:, 16:], right[:, :16, columns + TILE :]], axis=2),
    )
    got = send_both(((halves[0], "x"), (halves[1], "z")))
    far = send_on([((before[:4], after[4:]), axis) for (before, after), axis in zip(got, "xz")])
    held = [(halves[h], *got[h], *far[h]) for h in range(2)]

    *early, left = interleave(position, *held, columns, 0, 2)
    *late, weight = interleave(position, *held, columns, 2, chunks - 2, w_out)
    left_far = lax.ppermute(left, "x", ring(2))
    got = send_both(((early[0], "z"), (early[1], "x")))
    got, late, left_far = together((got, late, left_far))
    far = [lax.ppermute(before, axis, ring(1)) for (before, _), axis in zip(got, "zx")]
    after = [lax.ppermute(block, axis, ring(-1)) for block, axis in zip(late, "zx")]
    left = arrange_left(position, left, *got[1], left_far, 2 * 512)
    left = lax.all_gather(left, narrow, axis=0)
    far, late, left = together((far, late, left))
    early = [(early[h], *got[h], far[h]) for h in range(2)]
    before = [lax.ppermute(block, axis, ring(1)) for block, axis in zip(late, "zx")]
    left, after = together((left, after))
    far = [lax.ppermute(block, axis, ring(-1)) for block, axis in zip(after, "zx")]
    late = [(late[h], before[h], after[h], far[h]) for h in range(2)]

    result = pair(left, weight, *early, 0, 2, None, columns)
    return pair(left, weight, *late, 2, chunks - 2, result, columns)


def solution(mesh):
    split = Mesh(mesh.devices.reshape(4, 4, 2, 2, 2), EVERY)
    placed = (P(EVERY, None, None), P(EVERY, None)) + (P(),) * 7
    return jax.shard_map(
        on_device,
        mesh=split,
        in_specs=placed,
        out_specs=P(PLANE, ("yl", "core"), None),
        check_vma=False,
    )
```

```python
import jax
import jax.numpy as jnp
from jax import lax
from jax.experimental import pallas as pl
from jax.experimental.pallas import tpu as pltpu
from jax.sharding import Mesh
from jax.sharding import PartitionSpec as P

RD = 32
CHUNK = 256
GROUP = 32
TILE = 128
COLUMN = ("yh", "yl", "core")
PLANE = ("x", "z", "yh")
EVERY = ("x", "z", "yh", "yl", "core")
f32 = jnp.float32
bf16 = jnp.bfloat16


def vmem(mib=63):
    return pltpu.CompilerParams(vmem_limit_bytes=mib * 2**20)


def whole(*shape):
    return pl.BlockSpec(shape, lambda *_: (0,) * len(shape))


def turned(bias_ref):
    return jnp.broadcast_to(bias_ref[...], (8, bias_ref.shape[1])).T[:, :1]


def standardize(v, gain, bias):
    v = v.astype(f32)
    v = v - jnp.mean(v, axis=-1, keepdims=True)
    spread = jnp.mean(v * v, axis=-1, keepdims=True)
    return (v * lax.rsqrt(spread + 1e-05) * gain + bias).astype(bf16)


def affine(w_ref, bias, normed, mask):
    y = lax.dot_general(w_ref[...], normed, (((1,), (1,)), ((), ())), preferred_element_type=f32)
    return (y + bias) * mask


def one_hot(rows, columns, where):
    row = lax.broadcasted_iota(jnp.int32, (rows, columns), 0)
    column = lax.broadcasted_iota(jnp.int32, (rows, columns), 1)
    return jnp.where(where(row, column), 1.0, 0.0).astype(bf16)


def move(values, choose):
    return jnp.dot(values, choose, preferred_element_type=f32).astype(bf16)


def project(x, mask, gain, bias, w_left, b_left, w_right, b_right):
    rows, features = x.shape
    quarter = rows // 4
    width = w_right.shape[0]
    total = quarter + 2 * TILE
    left_rows = RD * 32
    sub = 640

    def kernel(x_ref, m_ref, g_ref, s_ref, wl_ref, bl_ref, wr_ref, br_ref, out_ref, normed, left, left_mask):
        step = pl.program_id(0)
        b = turned(br_ref)
        for part in range(quarter // sub):
            at = slice(part * sub, (part + 1) * sub)
            values = standardize(x_ref[at, :], g_ref[...], s_ref[...])
            normed[at, :] = values
            y = affine(wr_ref, b, values, m_ref[0, :, at]).astype(bf16)
            out_ref[0, 0, :, at] = y
            out_ref[1, 0, :, at] = y

        @pl.when(step == 0)
        def _():
            m = m_ref[0, :, :left_rows]
            y = affine(wl_ref, turned(bl_ref), normed[:left_rows, :], m)
            y = jnp.concatenate([y, jnp.broadcast_to(m, (16, left_rows))], axis=0).astype(bf16)

            def regroup(src, dst):
                return src == ((dst >> 3) & 3) * 64 + (dst >> 5) * 8 + (dst & 7)

            choose = one_hot(256, 256, regroup)
            y = [move(y[:, k * 256 : (k + 1) * 256], choose) for k in range(4)]
            for device in range(8):
                tile = jnp.concatenate([t[:, device * 32 : (device + 1) * 32] for t in y], axis=1)
                left[device] = tile[:width]
                left_mask[device] = tile[width:]

        m = [m_ref[0, :, k * TILE : (k + 1) * TILE] for k in range(quarter // TILE)]
        m = jnp.concatenate(m + [jnp.zeros((16 - len(m), TILE), f32)], axis=0).astype(bf16)
        for yh in range(2):
            device = yh * 4 + step
            out_ref[yh, 0, :16, quarter : quarter + TILE] = m
            out_ref[yh, 0, 16:, quarter : quarter + TILE] = left_mask[device]
            out_ref[yh, 0, :, quarter + TILE :] = left[device]

    return pl.pallas_call(
        kernel,
        grid=(4,),
        out_shape=jax.ShapeDtypeStruct((2, 4, width, total), bf16),
        in_specs=[
            pl.BlockSpec((quarter, features), lambda q: (q, 0)),
            pl.BlockSpec((1, 1, quarter), lambda q: (q, 0, 0)),
            whole(1, features),
            whole(1, features),
            whole(width, features),
            whole(1, width),
            whole(width, features),
            whole(1, width),
        ],
        out_specs=pl.BlockSpec((2, 1, width, total), lambda q: (0, q, 0, 0)),
        scratch_shapes=[
            pltpu.VMEM((quarter, features), bf16),
            pltpu.VMEM((8, width, TILE), bf16),
            pltpu.VMEM((8, 16, TILE), bf16),
        ],
        compiler_params=vmem(),
        name="project",
    )(x, mask.reshape(4, 1, quarter), gain, bias, w_left, b_left, w_right, b_right)


def ring(step):
    return [(i, (i + step) % 4) for i in range(4)]


def interleave(position, first, second, columns, start, chunks, w_out=None):
    tiles = CHUNK // TILE
    sizes = (8, 8, 8, 4, 4)
    heights = (544, 512)
    extra = 0 if w_out is not None else 144
    width = 32
    mask_tile = columns // TILE

    def by_row(ins, lane):
        own, before, after, low, high = ins
        at = slice(lane * TILE, (lane + 1) * TILE)
        parts = [own[:, :, at], before[:, :, at], after[:, :, at], low[:, :, at], high[:, :, at]]
        near = jnp.swapaxes(jnp.concatenate(parts[:2], axis=0), 0, 1)
        away = jnp.swapaxes(jnp.concatenate(parts[2:], axis=0), 0, 1)
        return jnp.concatenate([near, away], axis=1).reshape(512, TILE)

    def kernel(pos, *refs):
        main, masks, rest, outs = refs[:10], refs[10:15], refs[15:-3], refs[-3:]
        mask_rows = by_row(masks, 0)
        for chunk in range(chunks):
            for half in range(2):
                base = chunk * heights[half]
                for lane in range(tiles):
                    at = slice(lane * TILE, (lane + 1) * TILE)
                    rows = by_row(main[5 * half : 5 * half + 5], chunk * tiles + lane)
                    outs[half][base : base + 512, at] = rows
                    if half == 0:
                        row = ((start + chunk) * tiles + lane) * 32
                        outs[0][base + 512 : base + 544, at] = mask_rows[row : row + 32, :]
        if w_out is not None:
            w = rest[0][...].reshape(width, width, TILE)
            outs[2][...] = jnp.swapaxes(w, 0, 1).reshape(width * width, TILE).T
            return

        def mine(group):
            def pick(src, dst):
                place = ((dst >> 3) & 3) * 32 + pos[1] * 8 + (dst & 7)
                return (src == place) & ((dst >> 5) == group)

            return one_hot(TILE, TILE, pick)

        choose = [mine(group) for group in range(4)]
        left_masks, *lefts = [by_row(rest[5 * k : 5 * k + 5], 0) for k in range(3)]
        for lane, rows in enumerate(lefts):
            at = slice(lane * TILE, (lane + 1) * TILE)
            parts = [rows[g * 128 : (g + 1) * 128] for g in range(4)]
            parts = [jnp.dot(v, c, preferred_element_type=f32) for v, c in zip(parts, choose)]
            outs[2][:128, at] = sum(parts[1:], parts[0]).astype(bf16)
            outs[2][128:, at] = move(left_masks[lane * 16 : (lane + 1) * 16], choose[0])
        outs[1][chunks * 512 :, :] = outs[2][...]

    def blocks(m):
        span = chunks * CHUNK
        if start * CHUNK % span == 0:
            return pl.BlockSpec((m, 16, span), lambda _, pos: (0, 0, start * CHUNK // span))
        return pl.BlockSpec((pl.Element(m), pl.Element(16), pl.Element(span)), lambda _, pos: (0, 0, start * CHUNK))

    def tile_blocks(m, tile):
        return pl.BlockSpec((m, 16, TILE), lambda _, pos: (0, 0, tile))

    specs = [blocks(m) for m in sizes] * 2 + [tile_blocks(m, mask_tile) for m in sizes]
    args = (*first, *second, *first)
    shapes = [(chunks * heights[0], CHUNK), (chunks * heights[1] + extra, CHUNK)]
    if w_out is None:
        specs += [tile_blocks(m, mask_tile + k) for k in (0, 2, 1) for m in sizes]
        args += (*second, *second, *second)
        shapes.append((extra, CHUNK))
    else:
        specs.append(whole(*w_out.shape))
        args += (w_out,)
        shapes.append((w_out.shape[1], width * width))
    return pl.pallas_call(
        kernel,
        grid_spec=pltpu.PrefetchScalarGridSpec(
            num_scalar_prefetch=1,
            grid=(1,),
            in_specs=specs,
            out_specs=tuple(whole(*shape) for shape in shapes),
        ),
        out_shape=tuple(jax.ShapeDtypeStruct(shape, bf16) for shape in shapes),
        compiler_params=vmem(),
        name="interleave",
    )(position, *args)


def arrange_left(position, own, before, after, far, base):
    height = own.shape[0]

    def kernel(pos, *refs):
        ins, out_ref = refs[:4], refs[4]

        def sequences(rows, lane):
            return [r[rows, lane * TILE : (lane + 1) * TILE] for r in ins]

        def turn(choose, values):
            over = (((1,), (1,)), ((), ()))
            return lax.dot_general(choose, values, over, preferred_element_type=f32).astype(bf16)

        choose = one_hot(32, TILE, lambda row, lane: lane == (row & 3) * 32 + pos[0] * 8 + (row >> 2))
        held = []
        for lane in range(2):
            for c in range(4):
                values = jnp.concatenate(sequences(slice(c * 32, c * 32 + 32), lane), axis=0)
                held.append(turn(choose, values))

        def regroup(dst, src):
            c = dst & 31
            return src == (c >> 4) * 128 + (c & 3) * 32 + (dst >> 5) * 4 + ((c >> 2) & 3)

        held = move(one_hot(256, 256, regroup), jnp.concatenate(held, axis=0))
        swap = one_hot(128, 128, lambda k, to: to == ((k >> 3) & 3) * 32 + (k >> 5) * 8 + (k & 7))
        out_ref[:256, :] = move(held, swap)
        out_ref[256:512, :] = held
        masks = [sequences(slice(128, 144), lane) for lane in range(2)]
        masks = [masks[lane][place] for place in range(4) for lane in range(2)]
        choose = one_hot(16, TILE, lambda row, lane: lane == pos[0] * 8 + row)
        out_ref[512:, :] = move(turn(choose, jnp.concatenate(masks, axis=0)), swap)

    part = pl.BlockSpec((pl.Element(height), pl.Element(CHUNK)), lambda _, pos: (base, 0))
    return pl.pallas_call(
        kernel,
        grid_spec=pltpu.PrefetchScalarGridSpec(
            num_scalar_prefetch=1,
            grid=(1,),
            in_specs=[whole(*own.shape), part, part, whole(*far.shape)],
            out_specs=whole(528, 128),
        ),
        out_shape=jax.ShapeDtypeStruct((528, 128), bf16),
        compiler_params=vmem(),
        name="arrange_left",
    )(position, own, before, after, far)


def pair(left, weight, first, second, start, chunks, result, columns):
    out_width = weight.shape[0]
    earlier = () if result is None else (result,)

    def kernel(left_ref, w_ref, *refs):
        ins = refs[:8]
        out_ref, outer, scale, l1, l2, row_mask = refs[-6:]

        @pl.when(pl.program_id(0) == 0)
        def _():
            for device in range(4):
                at = slice(device * 256, (device + 1) * 256)
                l1[at, :] = left_ref[device, :256, :]
                l2[at, :] = left_ref[device, 256:512, :]
                row_mask[device * 8 : (device + 1) * 8, :] = left_ref[device, 512:, :].astype(f32)[:8]

        def sequences(half, row):
            at = slice(row * 32, row * 32 + 32)
            return jnp.concatenate([r[at, :] for r in ins[4 * half : 4 * half + 4]], axis=0)

        count = jnp.dot(row_mask[...].astype(bf16), sequences(0, 16), preferred_element_type=f32)
        scale[...] = 1.0 / (0.001 + count)

        def rows_of(group, _):
            at = pl.ds(pl.multiple_of(group * (GROUP * 32), GROUP * 32), GROUP * 32)
            for e in range(32):
                left = (l1, l2)[e // 16][at, :]
                prod = jnp.dot(left, sequences(e // 16, e % 16), preferred_element_type=f32).astype(bf16)
                for i in range(GROUP):
                    outer[i, e * 32 : (e + 1) * 32, :] = prod[i * 32 : (i + 1) * 32, :]
            part = scale[pl.ds(pl.multiple_of(group * GROUP, GROUP), GROUP), :]
            for i in range(GROUP):
                mixed = jnp.dot(w_ref[...], outer[i], preferred_element_type=f32)
                out_ref[group * GROUP + i] = (mixed * part[i : i + 1, :]).T.astype(bf16)
            return 0

        lax.fori_loop(0, RD // GROUP, rows_of, 0)

    blocks = [pl.BlockSpec((544, t.shape[1]), lambda j: (j, 0)) for t in first]
    blocks += [pl.BlockSpec((512, t.shape[1]), lambda j: (j, 0)) for t in second]
    return pl.pallas_call(
        kernel,
        grid=(chunks,),
        out_shape=jax.ShapeDtypeStruct((RD, columns, out_width), bf16),
        in_specs=[whole(*left.shape), whole(*weight.shape)]
        + blocks
        + [pl.BlockSpec(memory_space=pl.ANY)] * len(earlier),
        out_specs=pl.BlockSpec((RD, CHUNK, out_width), lambda j: (0, start + j, 0)),
        scratch_shapes=[
            pltpu.VMEM((GROUP, 1024, CHUNK), bf16),
            pltpu.VMEM((RD, CHUNK), f32),
            pltpu.VMEM((1024, 128), bf16),
            pltpu.VMEM((1024, 128), bf16),
            pltpu.VMEM((RD, 128), f32),
        ],
        input_output_aliases={10: 0} if earlier else {},
        compiler_params=vmem(),
        name="pair",
    )(left, weight, *first, *second, *earlier)


def send_both(blocks):
    return [
        (lax.ppermute(block, axis, ring(1)), lax.ppermute(block, axis, ring(-1))) for block, axis in blocks
    ]


def send_on(parts):
    return [
        (lax.ppermute(low, axis, ring(1)), lax.ppermute(high, axis, ring(-1))) for (low, high), axis in parts
    ]


def on_device(x, mask, gain, bias, w_left, b_left, w_right, b_right, w_out):
    columns = x.shape[1] // 4
    width = w_left.shape[1]
    chunks = columns // CHUNK
    together = lax.optimization_barrier

    narrow = ("yl", "core")
    position = jnp.stack([lax.axis_index(axis) for axis in ("x", "z")]).astype(jnp.int32)
    norm = gain[None], bias[None]
    right = project(x[0], mask, *norm, w_left.T, b_left[None], w_right.T, b_right[None])
    right = lax.all_to_all(right.reshape(8, width, -1), COLUMN, 0, 0, tiled=True)

    halves = (
        right[:, :16, : columns + TILE],
        jnp.concatenate([right[:, 16:], right[:, :16, columns + TILE :]], axis=2),
    )
    got = send_both(((halves[0], "x"), (halves[1], "z")))
    far = send_on([((before[:4], after[4:]), axis) for (before, after), axis in zip(got, "xz")])
    held = [(halves[h], *got[h], *far[h]) for h in range(2)]

    *early, left = interleave(position, *held, columns, 0, 2)
    *late, weight = interleave(position, *held, columns, 2, chunks - 2, w_out)
    left_far = lax.ppermute(left, "x", ring(2))
    got = send_both(((early[0], "z"), (early[1], "x")))
    got, late, left_far = together((got, late, left_far))
    far = [lax.ppermute(before, axis, ring(1)) for (before, _), axis in zip(got, "zx")]
    after = [lax.ppermute(block, axis, ring(-1)) for block, axis in zip(late, "zx")]
    left = arrange_left(position, left, *got[1], left_far, 2 * 512)
    left = lax.all_gather(left, narrow, axis=0)
    far, late, left = together((far, late, left))
    early = [(early[h], *got[h], far[h]) for h in range(2)]
    before = [lax.ppermute(block, axis, ring(1)) for block, axis in zip(late, "zx")]
    left, after = together((left, after))
    far = [lax.ppermute(block, axis, ring(-1)) for block, axis in zip(after, "zx")]
    late = [(late[h], before[h], after[h], far[h]) for h in range(2)]

    result = pair(left, weight, *early, 0, 2, None, columns)
    return pair(left, weight, *late, 2, chunks - 2, result, columns)


def solution(mesh):
    split = Mesh(mesh.devices.reshape(4, 4, 2, 2, 2), EVERY)
    placed = (P(EVERY, None, None), P(EVERY, None)) + (P(),) * 7
    return jax.shard_map(
        on_device,
        mesh=split,
        in_specs=placed,
        out_specs=P(PLANE, ("yl", "core"), None),
        check_vma=False,
    )
```

```python
import jax
import jax.numpy as jnp
from jax import lax
from jax.experimental import pallas as pl
from jax.experimental.pallas import tpu as pltpu
from jax.sharding import Mesh
from jax.sharding import PartitionSpec as P

RD = 32
CHUNK = 256
GROUP = 32
TILE = 128
COLUMN = ("yh", "yl", "core")
PLANE = ("x", "z", "yh")
EVERY = ("x", "z", "yh", "yl", "core")
f32 = jnp.float32
bf16 = jnp.bfloat16


def vmem(mib=63):
    return pltpu.CompilerParams(vmem_limit_bytes=mib * 2**20)


def whole(*shape):
    return pl.BlockSpec(shape, lambda *_: (0,) * len(shape))


def turned(bias_ref):
    return jnp.broadcast_to(bias_ref[...], (8, bias_ref.shape[1])).T[:, :1]


def standardize(v, gain, bias):
    v = v.astype(f32)
    v = v - jnp.mean(v, axis=-1, keepdims=True)
    spread = jnp.mean(v * v, axis=-1, keepdims=True)
    return (v * lax.rsqrt(spread + 1e-05) * gain + bias).astype(bf16)


def affine(w_ref, bias, normed, mask):
    y = lax.dot_general(w_ref[...], normed, (((1,), (1,)), ((), ())), preferred_element_type=f32)
    return (y + bias) * mask


def one_hot(rows, columns, where):
    row = lax.broadcasted_iota(jnp.int32, (rows, columns), 0)
    column = lax.broadcasted_iota(jnp.int32, (rows, columns), 1)
    return jnp.where(where(row, column), 1.0, 0.0).astype(bf16)


def move(values, choose):
    return jnp.dot(values, choose, preferred_element_type=f32).astype(bf16)


def project(x, mask, gain, bias, w_left, b_left, w_right, b_right):
    rows, features = x.shape
    quarter = rows // 4
    width = w_right.shape[0]
    total = quarter + 2 * TILE
    left_rows = RD * 32
    sub = 640

    def kernel(x_ref, m_ref, g_ref, s_ref, wl_ref, bl_ref, wr_ref, br_ref, out_ref, normed, left, left_mask):
        step = pl.program_id(0)
        b = turned(br_ref)
        for part in range(quarter // sub):
            at = slice(part * sub, (part + 1) * sub)
            values = standardize(x_ref[at, :], g_ref[...], s_ref[...])
            normed[at, :] = values
            y = affine(wr_ref, b, values, m_ref[0, :, at]).astype(bf16)
            out_ref[0, 0, :, at] = y
            out_ref[1, 0, :, at] = y

        @pl.when(step == 0)
        def _():
            m = m_ref[0, :, :left_rows]
            y = affine(wl_ref, turned(bl_ref), normed[:left_rows, :], m).astype(bf16)
            for yh in range(2):
                first = [(x * 8 + z * 2 + yh) * RD for x in range(4) for z in range(4)]
                pieces = [m[:, at : at + RD] for at in first]
                lines = [jnp.concatenate(pieces[4 * x : 4 * x + 4], axis=1) for x in range(4)]
                left_mask[yh] = jnp.concatenate(lines + [jnp.zeros((4, TILE), f32)], axis=0)

            def regroup(src, dst):
                return src == ((dst >> 3) & 3) * 64 + (dst >> 5) * 8 + (dst & 7)

            choose = one_hot(256, 256, regroup)
            y = [move(y[:, k * 256 : (k + 1) * 256], choose) for k in range(4)]
            for device in range(8):
                tile = jnp.concatenate([t[:, device * 32 : (device + 1) * 32] for t in y], axis=1)
                left[device] = tile

        m = [m_ref[0, :, k * TILE : (k + 1) * TILE] for k in range(quarter // TILE)]
        zeros = jnp.zeros((width - 4 - len(m), TILE), f32)
        for yh in range(2):
            tile = jnp.concatenate(m + [left_mask[yh, :4, :], zeros], axis=0)
            out_ref[yh, 0, :, quarter : quarter + TILE] = tile.astype(bf16)
            out_ref[yh, 0, :, quarter + TILE :] = left[yh * 4 + step]

    return pl.pallas_call(
        kernel,
        grid=(4,),
        out_shape=jax.ShapeDtypeStruct((2, 4, width, total), bf16),
        in_specs=[
            pl.BlockSpec((quarter, features), lambda q: (q, 0)),
            pl.BlockSpec((1, 1, quarter), lambda q: (q, 0, 0)),
            whole(1, features),
            whole(1, features),
            whole(width, features),
            whole(1, width),
            whole(width, features),
            whole(1, width),
        ],
        out_specs=pl.BlockSpec((2, 1, width, total), lambda q: (0, q, 0, 0)),
        scratch_shapes=[
            pltpu.VMEM((quarter, features), bf16),
            pltpu.VMEM((8, width, TILE), bf16),
            pltpu.VMEM((2, 8, TILE), f32),
        ],
        compiler_params=vmem(),
        name="project",
    )(x, mask.reshape(4, 1, quarter), gain, bias, w_left, b_left, w_right, b_right)


def ring(step):
    return [(i, (i + step) % 4) for i in range(4)]


def interleave(position, first, second, columns, start, chunks, w_out=None):
    tiles = CHUNK // TILE
    sizes = [[t.shape[0] for t in held] for held in (first, second)]
    cut = len(first)
    heights = (544, 512)
    extra = (16, 128) if w_out is None else (0, 0)
    width = 32
    mask_tile = columns // TILE

    def by_row(ins, lane):
        at = slice(lane * TILE, (lane + 1) * TILE)
        parts = [r[:, :, at] for r in ins]
        near = jnp.swapaxes(jnp.concatenate(parts[:2], axis=0), 0, 1)
        away = jnp.swapaxes(jnp.concatenate(parts[2:], axis=0), 0, 1)
        return jnp.concatenate([near, away], axis=1).reshape(512, TILE)

    def kernel(pos, *refs):
        n = cut + len(second)
        halves, masks = (refs[:cut], refs[cut:n]), refs[n : n + cut]
        rest, outs = refs[n + cut : -1 - len(shapes)], refs[-1 - len(shapes) : -1]
        mask_rows = refs[-1]
        mask_rows[...] = by_row(masks, 0)
        for chunk in range(chunks):
            for half in range(2):
                base = chunk * heights[half]
                for lane in range(tiles):
                    at = slice(lane * TILE, (lane + 1) * TILE)
                    rows = by_row(halves[half], chunk * tiles + lane)
                    outs[half][base : base + 512, at] = rows
                    if half == 0:
                        row = ((start + chunk) * tiles + lane) * 32
                        outs[0][base + 512 : base + 544, at] = mask_rows[row : row + 32, :]
        if w_out is not None:
            w = rest[0][...].reshape(width, width, TILE)
            outs[2][...] = jnp.swapaxes(w, 0, 1).reshape(width * width, TILE).T
            return

        def mine(group):
            def pick(src, dst):
                place = ((dst >> 3) & 3) * 32 + pos[1] * 8 + (dst & 7)
                return (src == place) & ((dst >> 5) == group)

            return one_hot(TILE, TILE, pick)

        choose = [mine(group) for group in range(4)]
        n = len(second)
        for lane in range(2):
            at = slice(lane * TILE, (lane + 1) * TILE)
            rows = by_row(rest[n * lane : n * lane + n], 0)
            parts = [rows[g * 128 : (g + 1) * 128] for g in range(4)]
            parts = [jnp.dot(v, c, preferred_element_type=f32) for v, c in zip(parts, choose)]
            outs[2][:, at] = sum(parts[1:], parts[0]).astype(bf16)
            row = (mask_tile + pos[0]) * 32 + lane * 16
            outs[0][chunks * heights[0] :, at] = mask_rows[pl.ds(pl.multiple_of(row, 16), 16), :]
        outs[1][chunks * heights[1] :, :] = outs[2][...]
        outs[3][...] = one_hot(RD, TILE, lambda row, lane: lane == pos[1] * RD + row)

    def blocks(m):
        span = chunks * CHUNK
        if start * CHUNK % span == 0:
            return pl.BlockSpec((m, 16, span), lambda _, pos: (0, 0, start * CHUNK // span))
        return pl.BlockSpec((pl.Element(m), pl.Element(16), pl.Element(span)), lambda _, pos: (0, 0, start * CHUNK))

    def tile_blocks(m, tile):
        return pl.BlockSpec((m, 16, TILE), lambda _, pos: (0, 0, tile))

    specs = [blocks(m) for held in sizes for m in held] + [tile_blocks(m, mask_tile) for m in sizes[0]]
    args = (*first, *second, *first)
    shapes = [(chunks * heights[half] + extra[half], CHUNK) for half in range(2)]
    if w_out is None:
        specs += [tile_blocks(m, mask_tile + k) for k in (1, 0) for m in sizes[1]]
        args += (*second, *second)
        shapes += [(extra[1], CHUNK), (RD, TILE)]
    else:
        specs.append(whole(*w_out.shape))
        args += (w_out,)
        shapes.append((w_out.shape[1], width * width))
    return pl.pallas_call(
        kernel,
        grid_spec=pltpu.PrefetchScalarGridSpec(
            num_scalar_prefetch=1,
            grid=(1,),
            in_specs=specs,
            out_specs=tuple(whole(*shape) for shape in shapes),
            scratch_shapes=[pltpu.VMEM((512, TILE), bf16)],
        ),
        out_shape=tuple(jax.ShapeDtypeStruct(shape, bf16) for shape in shapes),
        compiler_params=vmem(),
        name="interleave",
    )(position, *args)


def arrange_left(position, own, before, after, far, base):
    height = own.shape[0]

    def kernel(pos, *refs):
        ins, out_ref = refs[:4], refs[4]

        def sequences(rows, lane):
            return [r[rows, lane * TILE : (lane + 1) * TILE] for r in ins]

        def turn(choose, values):
            over = (((1,), (1,)), ((), ()))
            return lax.dot_general(choose, values, over, preferred_element_type=f32).astype(bf16)

        choose = one_hot(32, TILE, lambda row, lane: lane == (row & 3) * 32 + pos[0] * 8 + (row >> 2))
        held = []
        for lane in range(2):
            for c in range(4):
                values = jnp.concatenate(sequences(slice(c * 32, c * 32 + 32), lane), axis=0)
                held.append(turn(choose, values))

        def regroup(dst, src):
            c = dst & 31
            return src == (c >> 4) * 128 + (c & 3) * 32 + (dst >> 5) * 4 + ((c >> 2) & 3)

        out_ref[...] = move(one_hot(256, 256, regroup), jnp.concatenate(held, axis=0))

    part = pl.BlockSpec((pl.Element(height), pl.Element(CHUNK)), lambda _, pos: (base, 0))
    return pl.pallas_call(
        kernel,
        grid_spec=pltpu.PrefetchScalarGridSpec(
            num_scalar_prefetch=1,
            grid=(1,),
            in_specs=[whole(*own.shape), part, part, whole(*far.shape)],
            out_specs=whole(256, 128),
        ),
        out_shape=jax.ShapeDtypeStruct((256, 128), bf16),
        compiler_params=vmem(),
        name="arrange_left",
    )(position, own, before, after, far)


def pair(left, weight, mine, masks, first, second, start, chunks, result, columns):
    out_width = weight.shape[0]
    earlier = () if result is None else (result,)

    def kernel(left_ref, w_ref, mine_ref, *refs):
        mask_refs, ins = refs[:4], refs[4:12]
        out_ref, outer, scale, l1, l2, row_mask = refs[-6:]

        @pl.when(pl.program_id(0) == 0)
        def _():
            l2[...] = left_ref[...].reshape(RD * 32, 128)
            swap = one_hot(128, 128, lambda k, to: to == ((k >> 3) & 3) * 32 + (k >> 5) * 8 + (k & 7))
            l1[...] = move(l2[...], swap)
            parts = [r[:, lane * TILE : (lane + 1) * TILE] for r in mask_refs for lane in range(2)]
            row_mask[...] = lax.dot_general(
                mine_ref[...], jnp.concatenate(parts, axis=0), (((1,), (1,)), ((), ())),
                preferred_element_type=f32,
            ).astype(bf16)

        def sequences(half, row):
            at = slice(row * 32, row * 32 + 32)
            return jnp.concatenate([r[at, :] for r in ins[4 * half : 4 * half + 4]], axis=0)

        count = jnp.dot(row_mask[...], sequences(0, 16), preferred_element_type=f32)
        scale[...] = 1.0 / (0.001 + count)

        def rows_of(group, _):
            at = pl.ds(pl.multiple_of(group * (GROUP * 32), GROUP * 32), GROUP * 32)
            for e in range(32):
                left = (l1, l2)[e // 16][at, :]
                prod = jnp.dot(left, sequences(e // 16, e % 16), preferred_element_type=f32).astype(bf16)
                for i in range(GROUP):
                    outer[i, e * 32 : (e + 1) * 32, :] = prod[i * 32 : (i + 1) * 32, :]
            part = scale[pl.ds(pl.multiple_of(group * GROUP, GROUP), GROUP), :]
            for i in range(GROUP):
                mixed = jnp.dot(w_ref[...], outer[i], preferred_element_type=f32)
                out_ref[group * GROUP + i] = (mixed * part[i : i + 1, :]).T.astype(bf16)
            return 0

        lax.fori_loop(0, RD // GROUP, rows_of, 0)

    blocks = [pl.BlockSpec((544, t.shape[1]), lambda j: (j, 0)) for t in first]
    blocks += [pl.BlockSpec((512, t.shape[1]), lambda j: (j, 0)) for t in second]
    return pl.pallas_call(
        kernel,
        grid=(chunks,),
        out_shape=jax.ShapeDtypeStruct((RD, columns, out_width), bf16),
        in_specs=[whole(*left.shape), whole(*weight.shape), whole(*mine.shape)]
        + [pl.BlockSpec((16, CHUNK), lambda j: (2 * 544 // 16, 0))] * 4
        + blocks
        + [pl.BlockSpec(memory_space=pl.ANY)] * len(earlier),
        out_specs=pl.BlockSpec((RD, CHUNK, out_width), lambda j: (0, start + j, 0)),
        scratch_shapes=[
            pltpu.VMEM((GROUP, 1024, CHUNK), bf16),
            pltpu.VMEM((RD, CHUNK), f32),
            pltpu.VMEM((1024, 128), bf16),
            pltpu.VMEM((1024, 128), bf16),
            pltpu.VMEM((RD, 128), bf16),
        ],
        input_output_aliases={15: 0} if earlier else {},
        compiler_params=vmem(),
        name="pair",
    )(left, weight, mine, *masks, *first, *second, *earlier)


def send_both(blocks):
    return [
        (lax.ppermute(block, axis, ring(1)), lax.ppermute(block, axis, ring(-1))) for block, axis in blocks
    ]


def send_on(parts):
    return [
        (lax.ppermute(low, axis, ring(1)), lax.ppermute(high, axis, ring(-1))) for (low, high), axis in parts
    ]


def on_device(x, mask, gain, bias, w_left, b_left, w_right, b_right, w_out):
    columns = x.shape[1] // 4
    width = w_left.shape[1]
    chunks = columns // CHUNK
    together = lax.optimization_barrier

    narrow = ("yl", "core")
    position = jnp.stack([lax.axis_index(axis) for axis in ("x", "z")]).astype(jnp.int32)
    norm = gain[None], bias[None]
    right = project(x[0], mask, *norm, w_left.T, b_left[None], w_right.T, b_right[None])
    right = lax.all_to_all(right.reshape(8, width, -1), COLUMN, 0, 0, tiled=True)

    halves = (
        right[:, :16, : columns + TILE],
        jnp.concatenate(
            [right[:, 16:, :columns], right[:, 16:, columns + TILE :], right[:, :16, columns + TILE :]], axis=2
        ),
    )
    got = send_both(((halves[0], "x"), (halves[1], "z")))
    far = lax.ppermute(got[0][0], "x", ring(1))
    before, after = got[1]
    (passed,) = send_on([((before[:4], after[4:]), "z")])
    held = (halves[0], *got[0], far), (halves[1], before, after, *passed)

    *early, left, mine = interleave(position, *held, columns, 0, 2)
    *late, weight = interleave(position, *held, columns, 2, chunks - 2, w_out)
    left_far = lax.ppermute(left, "x", ring(2))
    got = send_both(((early[0], "z"), (early[1], "x")))
    got, late, left_far = together((got, late, left_far))
    far = [lax.ppermute(before, axis, ring(1)) for (before, _), axis in zip(got, "zx")]
    after = [lax.ppermute(block, axis, ring(-1)) for block, axis in zip(late, "zx")]
    left = arrange_left(position, left, *got[1], left_far, 2 * 512)
    left = lax.all_gather(left, narrow, axis=0)
    far, late, left = together((far, late, left))
    early = [(early[h], *got[h], far[h]) for h in range(2)]
    before = [lax.ppermute(block, axis, ring(1)) for block, axis in zip(late, "zx")]
    left, after = together((left, after))
    far = [lax.ppermute(block, axis, ring(-1)) for block, axis in zip(after, "zx")]
    late = [(late[h], before[h], after[h], far[h]) for h in range(2)]

    fixed = left, weight, mine, early[0]
    result = pair(*fixed, *early, 0, 2, None, columns)
    return pair(*fixed, *late, 2, chunks - 2, result, columns)


def solution(mesh):
    split = Mesh(mesh.devices.reshape(4, 4, 2, 2, 2), EVERY)
    placed = (P(EVERY, None, None), P(EVERY, None)) + (P(),) * 7
    return jax.shard_map(
        on_device,
        mesh=split,
        in_specs=placed,
        out_specs=P(PLANE, ("yl", "core"), None),
        check_vma=False,
    )
```

```python
import jax
import jax.numpy as jnp
from jax import lax
from jax.experimental import pallas as pl
from jax.experimental.pallas import tpu as pltpu
from jax.sharding import Mesh
from jax.sharding import PartitionSpec as P

RD = 32
CHUNK = 256
GROUP = 32
TILE = 128
COLUMN = ("yh", "yl", "core")
PLANE = ("x", "z", "yh")
EVERY = ("x", "z", "yh", "yl", "core")
f32 = jnp.float32
bf16 = jnp.bfloat16


def vmem(mib=63):
    return pltpu.CompilerParams(vmem_limit_bytes=mib * 2**20)


def whole(*shape):
    return pl.BlockSpec(shape, lambda *_: (0,) * len(shape))


def turned(bias_ref):
    return jnp.broadcast_to(bias_ref[...], (8, bias_ref.shape[1])).T[:, :1]


def standardize(v, gain, bias):
    v = v.astype(f32)
    v = v - jnp.mean(v, axis=-1, keepdims=True)
    spread = jnp.mean(v * v, axis=-1, keepdims=True)
    return (v * lax.rsqrt(spread + 1e-05) * gain + bias).astype(bf16)


def affine(w_ref, bias, normed, mask):
    y = lax.dot_general(w_ref[...], normed, (((1,), (1,)), ((), ())), preferred_element_type=f32)
    return (y + bias) * mask


def one_hot(rows, columns, where):
    row = lax.broadcasted_iota(jnp.int32, (rows, columns), 0)
    column = lax.broadcasted_iota(jnp.int32, (rows, columns), 1)
    return jnp.where(where(row, column), 1.0, 0.0).astype(bf16)


def move(values, choose):
    return jnp.dot(values, choose, preferred_element_type=f32).astype(bf16)


def project(x, mask, gain, bias, w_left, b_left, w_right, b_right):
    rows, features = x.shape
    quarter = rows // 4
    width = w_right.shape[0]
    total = quarter + 2 * TILE
    left_rows = RD * 32
    sub = 640

    def kernel(x_ref, m_ref, g_ref, s_ref, wl_ref, bl_ref, wr_ref, br_ref, out_ref, normed, left, left_mask):
        step = pl.program_id(0)
        b = turned(br_ref)
        for part in range(quarter // sub):
            at = slice(part * sub, (part + 1) * sub)
            values = standardize(x_ref[at, :], g_ref[...], s_ref[...])
            normed[at, :] = values
            y = affine(wr_ref, b, values, m_ref[0, :, at]).astype(bf16)
            out_ref[0, 0, :, at] = y
            out_ref[1, 0, :, at] = y

        @pl.when(step == 0)
        def _():
            m = m_ref[0, :, :left_rows]
            y = affine(wl_ref, turned(bl_ref), normed[:left_rows, :], m).astype(bf16)
            for yh in range(2):
                first = [(x * 8 + z * 2 + yh) * RD for x in range(4) for z in range(4)]
                pieces = [m[:, at : at + RD] for at in first]
                lines = [jnp.concatenate(pieces[4 * x : 4 * x + 4], axis=1) for x in range(4)]
                left_mask[yh] = jnp.concatenate(lines + [jnp.zeros((4, TILE), f32)], axis=0)

            def regroup(src, dst):
                return src == ((dst >> 3) & 3) * 64 + (dst >> 5) * 8 + (dst & 7)

            choose = one_hot(256, 256, regroup)
            y = [move(y[:, k * 256 : (k + 1) * 256], choose) for k in range(4)]
            for device in range(8):
                tile = jnp.concatenate([t[:, device * 32 : (device + 1) * 32] for t in y], axis=1)
                left[device] = tile

        m = [m_ref[0, :, k * TILE : (k + 1) * TILE] for k in range(quarter // TILE)]
        zeros = jnp.zeros((width - 4 - len(m), TILE), f32)
        for yh in range(2):
            tile = jnp.concatenate(m + [left_mask[yh, :4, :], zeros], axis=0)
            out_ref[yh, 0, :, quarter : quarter + TILE] = tile.astype(bf16)
            out_ref[yh, 0, :, quarter + TILE :] = left[yh * 4 + step]

    return pl.pallas_call(
        kernel,
        grid=(4,),
        out_shape=jax.ShapeDtypeStruct((2, 4, width, total), bf16),
        in_specs=[
            pl.BlockSpec((quarter, features), lambda q: (q, 0)),
            pl.BlockSpec((1, 1, quarter), lambda q: (q, 0, 0)),
            whole(1, features),
            whole(1, features),
            whole(width, features),
            whole(1, width),
            whole(width, features),
            whole(1, width),
        ],
        out_specs=pl.BlockSpec((2, 1, width, total), lambda q: (0, q, 0, 0)),
        scratch_shapes=[
            pltpu.VMEM((quarter, features), bf16),
            pltpu.VMEM((8, width, TILE), bf16),
            pltpu.VMEM((2, 8, TILE), f32),
        ],
        compiler_params=vmem(),
        name="project",
    )(x, mask.reshape(4, 1, quarter), gain, bias, w_left, b_left, w_right, b_right)


def ring(step):
    return [(i, (i + step) % 4) for i in range(4)]


def interleave(position, first, second, columns, start, chunks, w_out=None):
    tiles = CHUNK // TILE
    sizes = [[t.shape[0] for t in held] for held in (first, second)]
    cut = len(first)
    heights = (544, 512)
    extra = (16, 128) if w_out is None else (0, 0)
    width = 32
    mask_tile = columns // TILE

    def by_row(ins, lane):
        at = slice(lane * TILE, (lane + 1) * TILE)
        parts = [r[:, :, at] for r in ins]
        near = jnp.swapaxes(jnp.concatenate(parts[:2], axis=0), 0, 1)
        away = jnp.swapaxes(jnp.concatenate(parts[2:], axis=0), 0, 1)
        return jnp.concatenate([near, away], axis=1).reshape(512, TILE)

    def kernel(pos, *refs):
        n = cut + len(second)
        halves, masks = (refs[:cut], refs[cut:n]), refs[n : n + cut]
        rest, outs = refs[n + cut : -1 - len(shapes)], refs[-1 - len(shapes) : -1]
        mask_rows = refs[-1]
        mask_rows[...] = by_row(masks, 0)
        for chunk in range(chunks):
            for half in range(2):
                base = chunk * heights[half]
                for lane in range(tiles):
                    at = slice(lane * TILE, (lane + 1) * TILE)
                    rows = by_row(halves[half], chunk * tiles + lane)
                    outs[half][base : base + 512, at] = rows
                    if half == 0:
                        row = ((start + chunk) * tiles + lane) * 32
                        outs[0][base + 512 : base + 544, at] = mask_rows[row : row + 32, :]
        if w_out is not None:
            w = rest[0][...].reshape(width, width, TILE)
            outs[2][...] = jnp.swapaxes(w, 0, 1).reshape(width * width, TILE).T
            return

        def mine(group):
            def pick(src, dst):
                place = ((dst >> 3) & 3) * 32 + pos[1] * 8 + (dst & 7)
                return (src == place) & ((dst >> 5) == group)

            return one_hot(TILE, TILE, pick)

        choose = [mine(group) for group in range(4)]
        n = len(second)
        for lane in range(2):
            at = slice(lane * TILE, (lane + 1) * TILE)
            rows = by_row(rest[n * lane : n * lane + n], 0)
            parts = [rows[g * 128 : (g + 1) * 128] for g in range(4)]
            parts = [jnp.dot(v, c, preferred_element_type=f32) for v, c in zip(parts, choose)]
            outs[2][:, at] = sum(parts[1:], parts[0]).astype(bf16)
            row = (mask_tile + pos[0]) * 32 + lane * 16
            outs[0][chunks * heights[0] :, at] = mask_rows[pl.ds(pl.multiple_of(row, 16), 16), :]
        outs[1][chunks * heights[1] :, :] = outs[2][...]
        outs[3][...] = one_hot(RD, TILE, lambda row, lane: lane == pos[1] * RD + row)

    def blocks(m):
        span = chunks * CHUNK
        if start * CHUNK % span == 0:
            return pl.BlockSpec((m, 16, span), lambda _, pos: (0, 0, start * CHUNK // span))
        return pl.BlockSpec((pl.Element(m), pl.Element(16), pl.Element(span)), lambda _, pos: (0, 0, start * CHUNK))

    def tile_blocks(m, tile):
        return pl.BlockSpec((m, 16, TILE), lambda _, pos: (0, 0, tile))

    specs = [blocks(m) for held in sizes for m in held] + [tile_blocks(m, mask_tile) for m in sizes[0]]
    args = (*first, *second, *first)
    shapes = [(chunks * heights[half] + extra[half], CHUNK) for half in range(2)]
    if w_out is None:
        specs += [tile_blocks(m, mask_tile + k) for k in (1, 0) for m in sizes[1]]
        args += (*second, *second)
        shapes += [(extra[1], CHUNK), (RD, TILE)]
    else:
        specs.append(whole(*w_out.shape))
        args += (w_out,)
        shapes.append((w_out.shape[1], width * width))
    return pl.pallas_call(
        kernel,
        grid_spec=pltpu.PrefetchScalarGridSpec(
            num_scalar_prefetch=1,
            grid=(1,),
            in_specs=specs,
            out_specs=tuple(whole(*shape) for shape in shapes),
            scratch_shapes=[pltpu.VMEM((512, TILE), bf16)],
        ),
        out_shape=tuple(jax.ShapeDtypeStruct(shape, bf16) for shape in shapes),
        compiler_params=vmem(24),
        name="interleave",
    )(position, *args)


def arrange_left(position, own, before, after, far, base):
    height = own.shape[0]

    def kernel(pos, *refs):
        ins, out_ref = refs[:4], refs[4]

        def sequences(rows, lane):
            return [r[rows, lane * TILE : (lane + 1) * TILE] for r in ins]

        def turn(choose, values):
            over = (((1,), (1,)), ((), ()))
            return lax.dot_general(choose, values, over, preferred_element_type=f32).astype(bf16)

        choose = one_hot(32, TILE, lambda row, lane: lane == (row & 3) * 32 + pos[0] * 8 + (row >> 2))
        held = []
        for lane in range(2):
            for c in range(4):
                values = jnp.concatenate(sequences(slice(c * 32, c * 32 + 32), lane), axis=0)
                held.append(turn(choose, values))

        def regroup(dst, src):
            c = dst & 31
            return src == (c >> 4) * 128 + (c & 3) * 32 + (dst >> 5) * 4 + ((c >> 2) & 3)

        out_ref[...] = move(one_hot(256, 256, regroup), jnp.concatenate(held, axis=0))

    part = pl.BlockSpec((pl.Element(height), pl.Element(CHUNK)), lambda _, pos: (base, 0))
    return pl.pallas_call(
        kernel,
        grid_spec=pltpu.PrefetchScalarGridSpec(
            num_scalar_prefetch=1,
            grid=(1,),
            in_specs=[whole(*own.shape), part, part, whole(*far.shape)],
            out_specs=whole(256, 128),
        ),
        out_shape=jax.ShapeDtypeStruct((256, 128), bf16),
        compiler_params=vmem(24),
        name="arrange_left",
    )(position, own, before, after, far)


def pair(left, weight, mine, masks, first, second, start, chunks, result, columns):
    out_width = weight.shape[0]
    earlier = () if result is None else (result,)

    def kernel(left_ref, w_ref, mine_ref, *refs):
        mask_refs, ins = refs[:4], refs[4:12]
        out_ref, outer, scale, l1, l2, row_mask = refs[-6:]

        @pl.when(pl.program_id(0) == 0)
        def _():
            l2[...] = left_ref[...].reshape(RD * 32, 128)
            swap = one_hot(128, 128, lambda k, to: to == ((k >> 3) & 3) * 32 + (k >> 5) * 8 + (k & 7))
            l1[...] = move(l2[...], swap)
            parts = [r[:, lane * TILE : (lane + 1) * TILE] for r in mask_refs for lane in range(2)]
            row_mask[...] = lax.dot_general(
                mine_ref[...], jnp.concatenate(parts, axis=0), (((1,), (1,)), ((), ())),
                preferred_element_type=f32,
            ).astype(bf16)

        def sequences(half, row):
            at = slice(row * 32, row * 32 + 32)
            return jnp.concatenate([r[at, :] for r in ins[4 * half : 4 * half + 4]], axis=0)

        count = jnp.dot(row_mask[...], sequences(0, 16), preferred_element_type=f32)
        scale[...] = 1.0 / (0.001 + count)

        def rows_of(group, _):
            at = pl.ds(pl.multiple_of(group * (GROUP * 32), GROUP * 32), GROUP * 32)
            for e in range(32):
                left = (l1, l2)[e // 16][at, :]
                prod = jnp.dot(left, sequences(e // 16, e % 16), preferred_element_type=f32).astype(bf16)
                for i in range(GROUP):
                    outer[i, e * 32 : (e + 1) * 32, :] = prod[i * 32 : (i + 1) * 32, :]
            part = scale[pl.ds(pl.multiple_of(group * GROUP, GROUP), GROUP), :]
            for i in range(GROUP):
                mixed = jnp.dot(w_ref[...], outer[i], preferred_element_type=f32)
                out_ref[group * GROUP + i] = (mixed * part[i : i + 1, :]).T.astype(bf16)
            return 0

        lax.fori_loop(0, RD // GROUP, rows_of, 0)

    blocks = [pl.BlockSpec((544, t.shape[1]), lambda j: (j, 0)) for t in first]
    blocks += [pl.BlockSpec((512, t.shape[1]), lambda j: (j, 0)) for t in second]
    return pl.pallas_call(
        kernel,
        grid=(chunks,),
        out_shape=jax.ShapeDtypeStruct((RD, columns, out_width), bf16),
        in_specs=[whole(*left.shape), whole(*weight.shape), whole(*mine.shape)]
        + [pl.BlockSpec((16, CHUNK), lambda j: (2 * 544 // 16, 0))] * 4
        + blocks
        + [pl.BlockSpec(memory_space=pl.ANY)] * len(earlier),
        out_specs=pl.BlockSpec((RD, CHUNK, out_width), lambda j: (0, start + j, 0)),
        scratch_shapes=[
            pltpu.VMEM((GROUP, 1024, CHUNK), bf16),
            pltpu.VMEM((RD, CHUNK), f32),
            pltpu.VMEM((1024, 128), bf16),
            pltpu.VMEM((1024, 128), bf16),
            pltpu.VMEM((RD, 128), bf16),
        ],
        input_output_aliases={15: 0} if earlier else {},
        compiler_params=vmem(),
        name="pair",
    )(left, weight, mine, *masks, *first, *second, *earlier)


def send_both(blocks):
    return [
        (lax.ppermute(block, axis, ring(1)), lax.ppermute(block, axis, ring(-1))) for block, axis in blocks
    ]


def send_on(parts):
    return [
        (lax.ppermute(low, axis, ring(1)), lax.ppermute(high, axis, ring(-1))) for (low, high), axis in parts
    ]


def on_device(x, mask, gain, bias, w_left, b_left, w_right, b_right, w_out):
    columns = x.shape[1] // 4
    width = w_left.shape[1]
    chunks = columns // CHUNK
    together = lax.optimization_barrier

    narrow = ("yl", "core")
    position = jnp.stack([lax.axis_index(axis) for axis in ("x", "z")]).astype(jnp.int32)
    norm = gain[None], bias[None]
    right = project(x[0], mask, *norm, w_left.T, b_left[None], w_right.T, b_right[None])
    right = lax.all_to_all(right.reshape(8, width, -1), COLUMN, 0, 0, tiled=True)

    halves = (
        right[:, :16, : columns + TILE],
        jnp.concatenate(
            [right[:, 16:, :columns], right[:, 16:, columns + TILE :], right[:, :16, columns + TILE :]], axis=2
        ),
    )
    got = send_both(((halves[0], "x"), (halves[1], "z")))
    far = lax.ppermute(got[0][0], "x", ring(1))
    before, after = got[1]
    (passed,) = send_on([((before[:4], after[4:]), "z")])
    held = (halves[0], *got[0], far), (halves[1], before, after, *passed)

    *early, left, mine = interleave(position, *held, columns, 0, 2)
    *late, weight = interleave(position, *held, columns, 2, chunks - 2, w_out)
    left_far = lax.ppermute(left, "x", ring(2))
    got = send_both(((early[0], "z"), (early[1], "x")))
    got, late, left_far = together((got, late, left_far))
    far = [lax.ppermute(before, axis, ring(1)) for (before, _), axis in zip(got, "zx")]
    after = [lax.ppermute(block, axis, ring(-1)) for block, axis in zip(late, "zx")]
    left = arrange_left(position, left, *got[1], left_far, 2 * 512)
    left = lax.all_gather(left, narrow, axis=0)
    far, late, left = together((far, late, left))
    early = [(early[h], *got[h], far[h]) for h in range(2)]
    before = [lax.ppermute(block, axis, ring(1)) for block, axis in zip(late, "zx")]
    left, after = together((left, after))
    far = [lax.ppermute(block, axis, ring(-1)) for block, axis in zip(after, "zx")]
    late = [(late[h], before[h], after[h], far[h]) for h in range(2)]

    fixed = left, weight, mine, early[0]
    result = pair(*fixed, *early, 0, 2, None, columns)
    return pair(*fixed, *late, 2, chunks - 2, result, columns)


def solution(mesh):
    split = Mesh(mesh.devices.reshape(4, 4, 2, 2, 2), EVERY)
    placed = (P(EVERY, None, None), P(EVERY, None)) + (P(),) * 7
    return jax.shard_map(
        on_device,
        mesh=split,
        in_specs=placed,
        out_specs=P(PLANE, ("yl", "core"), None),
        check_vma=False,
    )
```

```python
import jax
import jax.numpy as jnp
from jax import lax
from jax.experimental import pallas as pl
from jax.experimental.pallas import tpu as pltpu
from jax.sharding import Mesh
from jax.sharding import PartitionSpec as P

RD = 32
CHUNK = 256
GROUP = 32
TILE = 128
COLUMN = ("yh", "yl", "core")
PLANE = ("x", "z", "yh")
EVERY = ("x", "z", "yh", "yl", "core")
f32 = jnp.float32
bf16 = jnp.bfloat16


def vmem(mib=63):
    return pltpu.CompilerParams(vmem_limit_bytes=mib * 2**20)


def whole(*shape):
    return pl.BlockSpec(shape, lambda *_: (0,) * len(shape))


def turned(bias_ref):
    return jnp.broadcast_to(bias_ref[...], (8, bias_ref.shape[1])).T[:, :1]


def standardize(v, gain, bias):
    v = v.astype(f32)
    v = v - jnp.mean(v, axis=-1, keepdims=True)
    spread = jnp.mean(v * v, axis=-1, keepdims=True)
    return (v * lax.rsqrt(spread + 1e-05) * gain + bias).astype(bf16)


def affine(w_ref, bias, normed, mask):
    y = lax.dot_general(w_ref[...], normed, (((1,), (1,)), ((), ())), preferred_element_type=f32)
    return (y + bias) * mask


def one_hot(rows, columns, where):
    row = lax.broadcasted_iota(jnp.int32, (rows, columns), 0)
    column = lax.broadcasted_iota(jnp.int32, (rows, columns), 1)
    return jnp.where(where(row, column), 1.0, 0.0).astype(bf16)


def move(values, choose):
    return jnp.dot(values, choose, preferred_element_type=f32).astype(bf16)


def project(x, mask, gain, bias, w_left, b_left, w_right, b_right):
    rows, features = x.shape
    quarter = rows // 4
    width = w_right.shape[0]
    total = quarter + 2 * TILE
    left_rows = RD * 32
    sub = 640

    def kernel(x_ref, m_ref, g_ref, s_ref, wl_ref, bl_ref, wr_ref, br_ref, out_ref, normed, left, left_mask):
        step = pl.program_id(0)
        b = turned(br_ref)
        for part in range(quarter // sub):
            at = slice(part * sub, (part + 1) * sub)
            values = standardize(x_ref[at, :], g_ref[...], s_ref[...])
            normed[at, :] = values
            y = affine(wr_ref, b, values, m_ref[0, :, at]).astype(bf16)
            out_ref[0, 0, :, at] = y
            out_ref[1, 0, :, at] = y

        @pl.when(step == 0)
        def _():
            m = m_ref[0, :, :left_rows]
            y = affine(wl_ref, turned(bl_ref), normed[:left_rows, :], m).astype(bf16)
            for yh in range(2):
                first = [(x * 8 + z * 2 + yh) * RD for x in range(4) for z in range(4)]
                pieces = [m[:, at : at + RD] for at in first]
                lines = [jnp.concatenate(pieces[4 * x : 4 * x + 4], axis=1) for x in range(4)]
                left_mask[yh] = jnp.concatenate(lines + [jnp.zeros((4, TILE), f32)], axis=0)

            def regroup(src, dst):
                return src == ((dst >> 3) & 3) * 64 + (dst >> 5) * 8 + (dst & 7)

            choose = one_hot(256, 256, regroup)
            y = [move(y[:, k * 256 : (k + 1) * 256], choose) for k in range(4)]
            for device in range(8):
                tile = jnp.concatenate([t[:, device * 32 : (device + 1) * 32] for t in y], axis=1)
                left[device] = tile

        m = [m_ref[0, :, k * TILE : (k + 1) * TILE] for k in range(quarter // TILE)]
        zeros = jnp.zeros((width - 4 - len(m), TILE), f32)
        for yh in range(2):
            tile = jnp.concatenate(m + [left_mask[yh, :4, :], zeros], axis=0)
            out_ref[yh, 0, :, quarter : quarter + TILE] = tile.astype(bf16)
            out_ref[yh, 0, :, quarter + TILE :] = left[yh * 4 + step]

    return pl.pallas_call(
        kernel,
        grid=(4,),
        out_shape=jax.ShapeDtypeStruct((2, 4, width, total), bf16),
        in_specs=[
            pl.BlockSpec((quarter, features), lambda q: (q, 0)),
            pl.BlockSpec((1, 1, quarter), lambda q: (q, 0, 0)),
            whole(1, features),
            whole(1, features),
            whole(width, features),
            whole(1, width),
            whole(width, features),
            whole(1, width),
        ],
        out_specs=pl.BlockSpec((2, 1, width, total), lambda q: (0, q, 0, 0)),
        scratch_shapes=[
            pltpu.VMEM((quarter, features), bf16),
            pltpu.VMEM((8, width, TILE), bf16),
            pltpu.VMEM((2, 8, TILE), f32),
        ],
        compiler_params=vmem(),
        name="project",
    )(x, mask.reshape(4, 1, quarter), gain, bias, w_left, b_left, w_right, b_right)


def ring(step):
    return [(i, (i + step) % 4) for i in range(4)]


def interleave(position, first, second, columns, start, chunks, w_out=None):
    tiles = CHUNK // TILE
    sizes = [[t.shape[0] for t in held] for held in (first, second)]
    cut = len(first)
    heights = (544, 512)
    extra = (16, 128) if w_out is None else (0, 0)
    width = 32
    mask_tile = columns // TILE

    def by_row(ins, lane):
        at = slice(lane * TILE, (lane + 1) * TILE)
        parts = [r[:, :, at] for r in ins]
        near = jnp.swapaxes(jnp.concatenate(parts[:2], axis=0), 0, 1)
        away = jnp.swapaxes(jnp.concatenate(parts[2:], axis=0), 0, 1)
        return jnp.concatenate([near, away], axis=1).reshape(512, TILE)

    def kernel(pos, *refs):
        n = cut + len(second)
        halves, masks = (refs[:cut], refs[cut:n]), refs[n : n + cut]
        rest, outs = refs[n + cut : -1 - len(shapes)], refs[-1 - len(shapes) : -1]
        mask_rows = refs[-1]
        mask_rows[...] = by_row(masks, 0)
        for chunk in range(chunks):
            for half in range(2):
                base = chunk * heights[half]
                for lane in range(tiles):
                    at = slice(lane * TILE, (lane + 1) * TILE)
                    rows = by_row(halves[half], chunk * tiles + lane)
                    outs[half][base : base + 512, at] = rows
                    if half == 0:
                        row = ((start + chunk) * tiles + lane) * 32
                        outs[0][base + 512 : base + 544, at] = mask_rows[row : row + 32, :]
        if w_out is not None:
            w = rest[0][...].reshape(width, width, TILE)
            outs[2][...] = jnp.swapaxes(w, 0, 1).reshape(width * width, TILE).T
            return

        def mine(group):
            def pick(src, dst):
                place = ((dst >> 3) & 3) * 32 + pos[1] * 8 + (dst & 7)
                return (src == place) & ((dst >> 5) == group)

            return one_hot(TILE, TILE, pick)

        choose = [mine(group) for group in range(4)]
        n = len(second)
        for lane in range(2):
            at = slice(lane * TILE, (lane + 1) * TILE)
            rows = by_row(rest[n * lane : n * lane + n], 0)
            parts = [rows[g * 128 : (g + 1) * 128] for g in range(4)]
            parts = [jnp.dot(v, c, preferred_element_type=f32) for v, c in zip(parts, choose)]
            outs[2][:, at] = sum(parts[1:], parts[0]).astype(bf16)
            row = (mask_tile + pos[0]) * 32 + lane * 16
            outs[0][chunks * heights[0] :, at] = mask_rows[pl.ds(pl.multiple_of(row, 16), 16), :]
        outs[1][chunks * heights[1] :, :] = outs[2][...]
        outs[3][...] = one_hot(RD, TILE, lambda row, lane: lane == pos[1] * RD + row)

    def blocks(m):
        span = chunks * CHUNK
        if start * CHUNK % span == 0:
            return pl.BlockSpec((m, 16, span), lambda _, pos: (0, 0, start * CHUNK // span))
        return pl.BlockSpec((pl.Element(m), pl.Element(16), pl.Element(span)), lambda _, pos: (0, 0, start * CHUNK))

    def tile_blocks(m, tile):
        return pl.BlockSpec((m, 16, TILE), lambda _, pos: (0, 0, tile))

    specs = [blocks(m) for held in sizes for m in held] + [tile_blocks(m, mask_tile) for m in sizes[0]]
    args = (*first, *second, *first)
    shapes = [(chunks * heights[half] + extra[half], CHUNK) for half in range(2)]
    if w_out is None:
        specs += [tile_blocks(m, mask_tile + k) for k in (1, 0) for m in sizes[1]]
        args += (*second, *second)
        shapes += [(extra[1], CHUNK), (RD, TILE)]
    else:
        specs.append(whole(*w_out.shape))
        args += (w_out,)
        shapes.append((w_out.shape[1], width * width))
    return pl.pallas_call(
        kernel,
        grid_spec=pltpu.PrefetchScalarGridSpec(
            num_scalar_prefetch=1,
            grid=(1,),
            in_specs=specs,
            out_specs=tuple(whole(*shape) for shape in shapes),
            scratch_shapes=[pltpu.VMEM((512, TILE), bf16)],
        ),
        out_shape=tuple(jax.ShapeDtypeStruct(shape, bf16) for shape in shapes),
        compiler_params=vmem(24),
        name="interleave",
    )(position, *args)


def arrange_left(position, own, before, after, far, base):
    height = own.shape[0]

    def kernel(pos, *refs):
        ins, out_ref = refs[:4], refs[4]

        def sequences(rows, lane):
            return [r[rows, lane * TILE : (lane + 1) * TILE] for r in ins]

        def turn(choose, values):
            over = (((1,), (1,)), ((), ()))
            return lax.dot_general(choose, values, over, preferred_element_type=f32).astype(bf16)

        choose = one_hot(32, TILE, lambda row, lane: lane == (row & 3) * 32 + pos[0] * 8 + (row >> 2))
        held = []
        for lane in range(2):
            for c in range(4):
                values = jnp.concatenate(sequences(slice(c * 32, c * 32 + 32), lane), axis=0)
                held.append(turn(choose, values))

        def regroup(dst, src):
            c = dst & 31
            return src == (c >> 4) * 128 + (c & 3) * 32 + (dst >> 5) * 4 + ((c >> 2) & 3)

        out_ref[...] = move(one_hot(256, 256, regroup), jnp.concatenate(held, axis=0))

    part = pl.BlockSpec((pl.Element(height), pl.Element(CHUNK)), lambda _, pos: (base, 0))
    return pl.pallas_call(
        kernel,
        grid_spec=pltpu.PrefetchScalarGridSpec(
            num_scalar_prefetch=1,
            grid=(1,),
            in_specs=[whole(*own.shape), part, part, whole(*far.shape)],
            out_specs=whole(256, 128),
        ),
        out_shape=jax.ShapeDtypeStruct((256, 128), bf16),
        compiler_params=vmem(24),
        name="arrange_left",
    )(position, own, before, after, far)


def pair(left, weight, mine, masks, first, second, start, chunks, result, columns):
    out_width = weight.shape[0]
    earlier = () if result is None else (result,)

    def kernel(left_ref, w_ref, mine_ref, *refs):
        mask_refs, ins = refs[:4], refs[4:12]
        out_ref, outer, scale, l1, l2, row_mask = refs[-6:]

        @pl.when(pl.program_id(0) == 0)
        def _():
            l2[...] = left_ref[...].reshape(RD * 32, 128)
            swap = one_hot(128, 128, lambda k, to: to == ((k >> 3) & 3) * 32 + (k >> 5) * 8 + (k & 7))
            l1[...] = move(l2[...], swap)
            parts = [r[:, lane * TILE : (lane + 1) * TILE] for r in mask_refs for lane in range(2)]
            row_mask[...] = lax.dot_general(
                mine_ref[...], jnp.concatenate(parts, axis=0), (((1,), (1,)), ((), ())),
                preferred_element_type=f32,
            ).astype(bf16)

        def sequences(half, row):
            at = slice(row * 32, row * 32 + 32)
            return jnp.concatenate([r[at, :] for r in ins[4 * half : 4 * half + 4]], axis=0)

        count = jnp.dot(row_mask[...], sequences(0, 16), preferred_element_type=f32)
        scale[...] = 1.0 / (0.001 + count)

        def rows_of(group, _):
            at = pl.ds(pl.multiple_of(group * (GROUP * 32), GROUP * 32), GROUP * 32)
            for e in range(32):
                left = (l1, l2)[e // 16][at, :]
                prod = jnp.dot(left, sequences(e // 16, e % 16), preferred_element_type=f32).astype(bf16)
                for i in range(GROUP):
                    outer[i, e * 32 : (e + 1) * 32, :] = prod[i * 32 : (i + 1) * 32, :]
            part = scale[pl.ds(pl.multiple_of(group * GROUP, GROUP), GROUP), :]
            for i in range(GROUP):
                mixed = jnp.dot(w_ref[...], outer[i], preferred_element_type=f32)
                out_ref[group * GROUP + i] = (mixed * part[i : i + 1, :]).T.astype(bf16)
            return 0

        lax.fori_loop(0, RD // GROUP, rows_of, 0)

    blocks = [pl.BlockSpec((544, t.shape[1]), lambda j: (j, 0)) for t in first]
    blocks += [pl.BlockSpec((512, t.shape[1]), lambda j: (j, 0)) for t in second]
    return pl.pallas_call(
        kernel,
        grid=(chunks,),
        out_shape=jax.ShapeDtypeStruct((RD, columns, out_width), bf16),
        in_specs=[whole(*left.shape), whole(*weight.shape), whole(*mine.shape)]
        + [pl.BlockSpec((16, CHUNK), lambda j: (2 * 544 // 16, 0))] * 4
        + blocks
        + [pl.BlockSpec(memory_space=pl.ANY)] * len(earlier),
        out_specs=pl.BlockSpec((RD, CHUNK, out_width), lambda j: (0, start + j, 0)),
        scratch_shapes=[
            pltpu.VMEM((GROUP, 1024, CHUNK), bf16),
            pltpu.VMEM((RD, CHUNK), f32),
            pltpu.VMEM((1024, 128), bf16),
            pltpu.VMEM((1024, 128), bf16),
            pltpu.VMEM((RD, 128), bf16),
        ],
        input_output_aliases={15: 0} if earlier else {},
        compiler_params=vmem(40),
        name="pair",
    )(left, weight, mine, *masks, *first, *second, *earlier)


def send_both(blocks):
    return [
        (lax.ppermute(block, axis, ring(1)), lax.ppermute(block, axis, ring(-1))) for block, axis in blocks
    ]


def send_on(parts):
    return [
        (lax.ppermute(low, axis, ring(1)), lax.ppermute(high, axis, ring(-1))) for (low, high), axis in parts
    ]


def on_device(x, mask, gain, bias, w_left, b_left, w_right, b_right, w_out):
    columns = x.shape[1] // 4
    width = w_left.shape[1]
    chunks = columns // CHUNK
    together = lax.optimization_barrier

    narrow = ("yl", "core")
    position = jnp.stack([lax.axis_index(axis) for axis in ("x", "z")]).astype(jnp.int32)
    norm = gain[None], bias[None]
    right = project(x[0], mask, *norm, w_left.T, b_left[None], w_right.T, b_right[None])
    right = lax.all_to_all(right.reshape(8, width, -1), COLUMN, 0, 0, tiled=True)

    halves = (
        right[:, :16, : columns + TILE],
        jnp.concatenate(
            [right[:, 16:, :columns], right[:, 16:, columns + TILE :], right[:, :16, columns + TILE :]], axis=2
        ),
    )
    got = send_both(((halves[0], "x"), (halves[1], "z")))
    far = lax.ppermute(got[0][0], "x", ring(1))
    before, after = got[1]
    (passed,) = send_on([((before[:4], after[4:]), "z")])
    held = (halves[0], *got[0], far), (halves[1], before, after, *passed)

    *early, left, mine = interleave(position, *held, columns, 0, 2)
    *late, weight = interleave(position, *held, columns, 2, chunks - 2, w_out)
    left_far = lax.ppermute(left, "x", ring(2))
    got = send_both(((early[0], "z"), (early[1], "x")))
    got, late, left_far = together((got, late, left_far))
    far = [lax.ppermute(before, axis, ring(1)) for (before, _), axis in zip(got, "zx")]
    after = [lax.ppermute(block, axis, ring(-1)) for block, axis in zip(late, "zx")]
    left = arrange_left(position, left, *got[1], left_far, 2 * 512)
    left = lax.all_gather(left, narrow, axis=0)
    far, late, left = together((far, late, left))
    early = [(early[h], *got[h], far[h]) for h in range(2)]
    before = [lax.ppermute(block, axis, ring(1)) for block, axis in zip(late, "zx")]
    left, after = together((left, after))
    far = [lax.ppermute(block, axis, ring(-1)) for block, axis in zip(after, "zx")]
    late = [(late[h], before[h], after[h], far[h]) for h in range(2)]

    fixed = left, weight, mine, early[0]
    result = pair(*fixed, *early, 0, 2, None, columns)
    return pair(*fixed, *late, 2, chunks - 2, result, columns)


def solution(mesh):
    split = Mesh(mesh.devices.reshape(4, 4, 2, 2, 2), EVERY)
    placed = (P(EVERY, None, None), P(EVERY, None)) + (P(),) * 7
    return jax.shard_map(
        on_device,
        mesh=split,
        in_specs=placed,
        out_specs=P(PLANE, ("yl", "core"), None),
        check_vma=False,
    )
```
